32 devices in a mesh: tm: 8 (over z, y), row: 4 (over x, core).
Axes of the slice: x: 2, y: 2, z: 4, core: 2. Of those that a mesh axis runs over, the one named last changes fastest.
Arguments:
- latents: bfloat16 [16, 24, 80, 256], P('tm', 'row'), may hold values from -6 to 6
- conv_weight: bfloat16 [3, 3, 768, 256], replicated, may hold values from -0.078125 to 0.078125
- norm_gain: float32 [256], replicated, may hold values from 0.1 to 1.9
- depth_target: bfloat16 [16, 24, 80, 128], P('tm', 'row'), may hold values from -6 to 6
Outputs:
- features: bfloat16 [16, 24, 80, 256], P('tm', 'row')
- gram: float32 [256, 256], replicated
- cross: float32 [256, 128], replicated
The draws below stay inside these ranges and needn't reach their ends.
All inputs are finite; a program needn't handle non-finite values.
Results may differ from the reference program's by a relative error of at most 0.003.
Values may be sent and summed in bfloat16 or wider, within the bound.
No kernel may reach another device: no remote copies, remote signals or barrier semaphores. Data moves between devices by JAX's collectives and lax.ppermute only.
A program may use at most 64 MiB of HBM per device.

```python
import jax
import jax.numpy as jnp
from jax import lax

C = 256
BINS = 128
COLS = 80
FRAMES = 16
ROWS = 24


def levels(stream_key, dims, cuts, least, largest):
    def one(position, parts):
        draws = jax.random.uniform(jax.random.fold_in(jax.random.fold_in(stream_key, 6), position), (parts,), jnp.float32, least / len(cuts), largest / len(cuts))
        return jnp.repeat(jnp.exp(draws), dims[position] // parts).reshape((-1,) + (1,) * (len(dims) - position - 1))

    loudness = one(*cuts[0])
    for cut in cuts[1:]:
        loudness = loudness * one(*cut)
    return loudness


def centred(key, extent, deviation, most, cuts=(), kind=jnp.bfloat16):
    array = deviation * jax.random.normal(key, extent, jnp.float32)
    if cuts:
        array = array * levels(key, extent, cuts, -0.22, 0.18)
    return jnp.clip(array, -most, most).astype(kind)


def setup_inputs(seed: int = 0) -> dict:
    splits = jax.random.split(jax.random.key(seed), 5)
    latents = centred(splits[0], (FRAMES, ROWS, COLS, C), 1.0, 6.0, ((0, 8), (1, 4)))
    conv_weight = centred(splits[1], (3, 3, 3 * C, C), (27 * C) ** -0.5, 0.078125)
    norm_gain = jnp.clip(1.0 + 0.18 * jax.random.normal(splits[2], (C,), jnp.float32), 0.1, 1.9)
    depth_target = centred(splits[3], (FRAMES, ROWS, COLS, BINS), 1.0, 6.0, ((0, 8), (1, 4)))
    return {"latents": latents, "conv_weight": conv_weight, "norm_gain": norm_gain, "depth_target": depth_target}


def convolve(padded, conv_weight):
    frames = padded.shape[0] - 2
    rows = padded.shape[1] - 2
    cols = padded.shape[2]
    chans = conv_weight.shape[3]
    wide = jnp.pad(padded, ((0, 0), (0, 0), (1, 1), (0, 0)))
    stacked = jnp.concatenate([wide[:, :, 0:cols], wide[:, :, 1:cols + 1], wide[:, :, 2:cols + 2]], axis=3)
    total = jnp.zeros((frames * rows * cols, chans), jnp.float32)
    for dtime in range(3):
        for drow in range(3):
            piece = stacked[dtime:dtime + frames, drow:drow + rows].reshape(frames * rows * cols, -1)
            total = total + jnp.dot(piece, conv_weight[dtime, drow], preferred_element_type=jnp.float32)
    return total

def make_features(latents, conv, norm_gain):
    flat = latents.reshape(conv.shape[0], conv.shape[1]).astype(jnp.float32)
    normed = conv * jax.lax.rsqrt(lax.optimization_barrier(jnp.mean(conv * conv, axis=1, keepdims=True)) + 1e-06) * norm_gain
    return (flat + jax.nn.silu(normed)).astype(jnp.bfloat16)

def reference(latents, conv_weight, norm_gain, depth_target):
    padded = jnp.pad(latents, ((2, 0), (1, 1), (0, 0), (0, 0)))
    conv = convolve(padded, conv_weight)
    flat = make_features(latents, conv, norm_gain)
    targets = depth_target.reshape(flat.shape[0], -1)
    count = flat.shape[0]
    gram = jnp.dot(flat.T, flat, preferred_element_type=jnp.float32) / count
    cross = jnp.dot(flat.T, targets, preferred_element_type=jnp.float32) / count
    return (flat.reshape(latents.shape), gram, cross)
```

```python
import functools

import jax
import jax.numpy as jnp
from jax import lax
from jax.experimental import pallas as pl
from jax.experimental.pallas import tpu as pltpu
from jax.sharding import PartitionSpec as P

F32 = jnp.float32
BF16 = jnp.bfloat16
WHOLE = pl.BlockSpec(memory_space=pltpu.VMEM)


def params(mebibytes):
    return pltpu.CompilerParams(vmem_limit_bytes=mebibytes * 2**20)


def on_even_row():
    return lax.axis_index("row") % 2 == 0


def by_device(value, moves):
    rows = lax.axis_size("row")
    return lax.ppermute(value, ("tm", "row"), [(a * rows + b, c * rows + d) for (a, b), (c, d) in moves])


def later(value):
    return lax.ppermute(value, "tm", [(i, i + 1) for i in range(lax.axis_size("tm") - 1)])


def pick_kernel(old_edge_ref, edge_ref, mate_ref, cross_ref):
    def fill(to_mate, to_cross):
        for f in range(2):
            mate_ref[f] = old_edge_ref[f, to_mate]
            mate_ref[f + 2] = edge_ref[f, to_mate]
            cross_ref[f] = old_edge_ref[f, to_cross]
            cross_ref[f + 2] = edge_ref[f, to_cross]

    @pl.when(on_even_row())
    def _():
        fill(1, 0)

    @pl.when(jnp.logical_not(on_even_row()))
    def _():
        fill(0, 1)


def frame_rows(edge_ref, mid_ref, f):
    rows, cols, chans = mid_ref.shape[1:]
    return [edge_ref[f, 0], mid_ref[f].reshape(rows * cols, chans), edge_ref[f, 1]]


def column_taps(stacks, weight_ref, times, chans):
    rows = jnp.concatenate(stacks, axis=1)
    products = []
    for tap in range(3):
        weights = [weight_ref[t, dh, tap * chans : (tap + 1) * chans] for t in times for dh in range(3)]
        products.append(jnp.dot(rows, jnp.concatenate(weights, axis=0), preferred_element_type=F32))
    return products


def stacked_rows(rows, cols):
    wide = jnp.concatenate(rows, axis=0)
    span = wide.shape[0] - 2 * cols
    return jnp.concatenate([wide[tap * cols : tap * cols + span] for tap in range(3)], axis=1)


def joined_columns(products, cols):
    left, middle, right = products
    span = left.shape[0]
    col = lax.broadcasted_iota(jnp.int32, (span, 1), 0) % cols
    left = jnp.where(col == 0, 0.0, pltpu.roll(left, 1, 0))
    right = jnp.where(col == cols - 1, 0.0, pltpu.roll(right, span - 1, 0))
    return left + middle + right


def own_kernel(edge_ref, mid_ref, weight_ref, part_ref):
    cols, chans = edge_ref.shape[2:]
    span = part_ref.shape[0] // 2
    none = jnp.zeros((cols, chans), BF16)
    stacks = [stacked_rows([none, *frame_rows(edge_ref, mid_ref, f), none], cols) for f in range(2)]
    part_ref[:span] = joined_columns(column_taps(stacks[:1], weight_ref, [2], chans), cols)
    part_ref[span:] = joined_columns(column_taps(stacks, weight_ref, [1, 2], chans), cols)


def rest_kernel(edge_ref, mid_ref, old_edge_ref, old_mid_ref, mate_ref, cross_ref, weight_ref, part_ref,
                gain_ref, target_ref, feature_ref, keep_ref, send_ref):
    cols, chans = edge_ref.shape[2:]
    span, half = part_ref.shape[0] // 2, chans // 2
    even = on_even_row()
    above = [jnp.where(even, cross_ref[f], mate_ref[f]) for f in range(4)]
    below = [jnp.where(even, mate_ref[f], cross_ref[f]) for f in range(4)]
    stacks = []
    for f in range(2):
        stacks.append(stacked_rows([above[f], *frame_rows(old_edge_ref, old_mid_ref, f), below[f]], cols))
    halo = []
    for tap in range(3):
        here = slice(tap * chans, (tap + 1) * chans)
        for dh, rim in ((0, above), (2, below)):
            two = jnp.dot(jnp.concatenate(rim[2:], axis=0), weight_ref[2, dh, here], preferred_element_type=F32)
            one = jnp.dot(rim[2], weight_ref[1, dh, here], preferred_element_type=F32)
            halo.append((two[:cols], two[cols:] + one))
    for f in (1, 0):
        here = slice(f * span, (f + 1) * span)
        times = [0, 1] if f == 0 else [0]
        products = column_taps(stacks[f:], weight_ref, times, chans)
        for tap in range(3):
            whole = products[tap]
            parts = [whole[:cols] + halo[2 * tap][f], whole[cols : span - cols], whole[span - cols :] + halo[2 * tap + 1][f]]
            products[tap] = jnp.concatenate(parts, axis=0)
        conv = part_ref[here] + joined_columns(products, cols)
        mean = jnp.mean(conv * conv, axis=1, keepdims=True)
        normed = conv * lax.rsqrt(mean + 1e-06) * gain_ref[...]
        silu = 0.5 * normed * (1.0 + jnp.tanh(0.5 * normed))
        mine = jnp.concatenate(frame_rows(edge_ref, mid_ref, f), axis=0).astype(F32)
        feature_ref[here] = (mine + silu).astype(BF16)
    features = feature_ref[...]
    both = jnp.concatenate([features, target_ref[...]], axis=1)
    sums = jnp.dot(features.T, both, preferred_element_type=F32)
    cut = half // 2
    low = [sums[:half, :half], sums[:half, half:chans], sums[half : half + cut, half:chans]]
    high = [sums[:half, chans:], sums[half:, chans:], sums[half + cut :, half:chans]]
    low, high = jnp.concatenate(low, axis=0), jnp.concatenate(high, axis=0)

    @pl.when(even)
    def _():
        keep_ref[...] = low
        send_ref[...] = high

    @pl.when(jnp.logical_not(even))
    def _():
        keep_ref[...] = high
        send_ref[...] = low


def unpack_kernel(count, mine_ref, other_ref, gram_ref, cross_ref):
    half = mine_ref.shape[1]
    cut = half // 2

    def fill(low, high):
        corner = low[half : 2 * half] / count
        gram_ref[:half, :half] = low[:half] / count
        gram_ref[:half, half:] = corner
        gram_ref[half:, :half] = corner.T
        gram_ref[half : half + cut, half:] = low[2 * half :] / count
        gram_ref[half + cut :, half:] = high[2 * half :] / count
        cross_ref[...] = high[: 2 * half] / count

    @pl.when(on_even_row())
    def _():
        fill(mine_ref, other_ref)

    @pl.when(jnp.logical_not(on_even_row()))
    def _():
        fill(other_ref, mine_ref)


def total_over_chips(value):
    blocks, rows = lax.axis_size("tm"), lax.axis_size("row")
    steps = [("row", 2**k) for k in range(1, rows.bit_length() - 1)]
    steps += [("tm", 2**k) for k in range(blocks.bit_length() - 1)]
    for s in range(len(steps)):
        moves = []
        for a in range(blocks):
            for b in range(rows):
                swap = s ^ (b % 2)
                axis, bit = steps[swap if swap < len(steps) else s]
                moves.append(((a, b), (a ^ bit, b) if axis == "tm" else (a, b ^ bit)))
        value = value + by_device(value, moves)
    return value


def on_device(latents, conv_weight, norm_gain, depth_target):
    frames, rows, cols, chans = latents.shape
    spots = frames * rows * cols
    bins = depth_target.shape[3]
    half = chans // 2
    blocks, bands = lax.axis_size("tm"), lax.axis_size("row")
    edge = jnp.stack([latents[:, 0], latents[:, -1]], axis=1)
    mid = latents[:, 1:-1]
    old_edge = later(edge)
    old_mid = later(mid)
    rim = jax.ShapeDtypeStruct((2 * frames, cols, chans), BF16)
    mate, cross = pl.pallas_call(
        pick_kernel,
        out_shape=(rim, rim),
        in_specs=[WHOLE] * 2,
        out_specs=(WHOLE,) * 2,
        compiler_params=params(4),
        cost_estimate=pl.CostEstimate(flops=4 * 10**9, bytes_accessed=2**20, transcendentals=0),
    )(old_edge, edge)
    places = [(a, b) for a in range(blocks) for b in range(bands)]
    mate_rim = by_device(mate, [((a, b), (a, b ^ 1)) for a, b in places])
    pairs = [((a, b), (a, ((b + 1) ^ 1) - 1)) for a, b in places if 0 < b < bands - 1]
    cross_rim = by_device(cross, pairs)
    part = pl.pallas_call(
        own_kernel,
        out_shape=jax.ShapeDtypeStruct((spots, chans), F32),
        in_specs=[WHOLE] * 3,
        out_specs=WHOLE,
        compiler_params=params(24),
        cost_estimate=pl.CostEstimate(flops=spots * chans * chans * 27, bytes_accessed=5 * 2**20, transcendentals=0),
    )(edge, mid, conv_weight)
    features, keep, send = pl.pallas_call(
        rest_kernel,
        out_shape=(
            jax.ShapeDtypeStruct((spots, chans), BF16),
            jax.ShapeDtypeStruct((5 * half // 2, half), F32),
            jax.ShapeDtypeStruct((5 * half // 2, half), F32),
        ),
        in_specs=[WHOLE] * 10,
        out_specs=(WHOLE,) * 3,
        compiler_params=params(32),
        cost_estimate=pl.CostEstimate(flops=spots * chans * chans * 30, bytes_accessed=5 * 2**20, transcendentals=spots * chans),
    )(edge, mid, old_edge, old_mid, mate_rim, cross_rim, conv_weight, part,
      norm_gain.reshape(1, chans), depth_target.reshape(spots, bins))
    mine = total_over_chips(keep + by_device(send, [((a, b), (a, b ^ 1)) for a, b in places]))
    other = by_device(mine, [((a, b), (a, b ^ 1)) for a, b in places])
    gram, cross = pl.pallas_call(
        functools.partial(unpack_kernel, spots * blocks * bands),
        out_shape=(jax.ShapeDtypeStruct((chans, chans), F32), jax.ShapeDtypeStruct((chans, bins), F32)),
        in_specs=[WHOLE] * 2,
        out_specs=(WHOLE,) * 2,
        compiler_params=params(4),
    )(mine, other)
    return features.reshape(latents.shape), gram, cross


def solution(mesh):
    in_specs = (P("tm", "row", None, None), P(), P(), P("tm", "row", None, None))
    out_specs = (P("tm", "row", None, None), P(), P())
    return jax.shard_map(
        on_device, mesh=mesh, in_specs=in_specs, out_specs=out_specs, check_vma=False
    )
```

```python
import functools

import jax
import jax.numpy as jnp
from jax import lax
from jax.experimental import pallas as pl
from jax.experimental.pallas import tpu as pltpu
from jax.sharding import PartitionSpec as P

F32 = jnp.float32
BF16 = jnp.bfloat16
F16 = jnp.float16
HEAD = 16
WHOLE = pl.BlockSpec(memory_space=pltpu.VMEM)


def params(mebibytes):
    return pltpu.CompilerParams(vmem_limit_bytes=mebibytes * 2**20)


def on_even_row():
    return lax.axis_index("row") % 2 == 0


def by_device(value, moves):
    rows = lax.axis_size("row")
    return lax.ppermute(value, ("tm", "row"), [(a * rows + b, c * rows + d) for (a, b), (c, d) in moves])


def later(value):
    return lax.ppermute(value, "tm", [(i, i + 1) for i in range(lax.axis_size("tm") - 1)])


def pick_kernel(old_edge_ref, edge_ref, mate_ref, cross_ref):
    def fill(to_mate, to_cross):
        for f in range(2):
            mate_ref[f] = old_edge_ref[f, to_mate]
            mate_ref[f + 2] = edge_ref[f, to_mate]
            cross_ref[f] = old_edge_ref[f, to_cross]
            cross_ref[f + 2] = edge_ref[f, to_cross]

    @pl.when(on_even_row())
    def _():
        fill(1, 0)

    @pl.when(jnp.logical_not(on_even_row()))
    def _():
        fill(0, 1)


def frame_rows(edge_ref, mid_ref, f):
    rows, cols, chans = mid_ref.shape[1:]
    return [edge_ref[f, 0], mid_ref[f].reshape(rows * cols, chans), edge_ref[f, 1]]


def column_taps(stacks, weight_ref, times, chans):
    rows = jnp.concatenate(stacks, axis=1)
    products = []
    for tap in range(3):
        weights = [weight_ref[t, dh, tap * chans : (tap + 1) * chans] for t in times for dh in range(3)]
        products.append(jnp.dot(rows, jnp.concatenate(weights, axis=0), preferred_element_type=F32))
    return products


def stacked_rows(rows, cols):
    wide = jnp.concatenate(rows, axis=0)
    span = wide.shape[0] - 2 * cols
    return jnp.concatenate([wide[tap * cols : tap * cols + span] for tap in range(3)], axis=1)


def joined_columns(products, cols):
    left, middle, right = products
    span = left.shape[0]
    col = lax.broadcasted_iota(jnp.int32, (span, 1), 0) % cols
    left = jnp.where(col == 0, 0.0, pltpu.roll(left, 1, 0))
    right = jnp.where(col == cols - 1, 0.0, pltpu.roll(right, span - 1, 0))
    return left + middle + right


def own_kernel(edge_ref, mid_ref, weight_ref, part_ref):
    cols, chans = edge_ref.shape[2:]
    span = part_ref.shape[0] // 2
    none = jnp.zeros((cols, chans), BF16)
    stacks = [stacked_rows([none, *frame_rows(edge_ref, mid_ref, f), none], cols) for f in range(2)]
    part_ref[:span] = joined_columns(column_taps(stacks[:1], weight_ref, [2], chans), cols)
    part_ref[span:] = joined_columns(column_taps(stacks, weight_ref, [1, 2], chans), cols)


def rest_kernel(edge_ref, mid_ref, old_edge_ref, old_mid_ref, mate_ref, cross_ref, weight_ref, part_ref,
                gain_ref, target_ref, feature_ref, keep_ref, send_ref):
    cols, chans = edge_ref.shape[2:]
    span, half = part_ref.shape[0] // 2, chans // 2
    even = on_even_row()
    above = [jnp.where(even, cross_ref[f], mate_ref[f]) for f in range(4)]
    below = [jnp.where(even, mate_ref[f], cross_ref[f]) for f in range(4)]
    stacks = []
    for f in range(2):
        stacks.append(stacked_rows([above[f], *frame_rows(old_edge_ref, old_mid_ref, f), below[f]], cols))
    halo = []
    for tap in range(3):
        here = slice(tap * chans, (tap + 1) * chans)
        for dh, rim in ((0, above), (2, below)):
            two = jnp.dot(jnp.concatenate(rim[2:], axis=0), weight_ref[2, dh, here], preferred_element_type=F32)
            one = jnp.dot(rim[2], weight_ref[1, dh, here], preferred_element_type=F32)
            halo.append((two[:cols], two[cols:] + one))
    for f in (1, 0):
        here = slice(f * span, (f + 1) * span)
        times = [0, 1] if f == 0 else [0]
        products = column_taps(stacks[f:], weight_ref, times, chans)
        for tap in range(3):
            whole = products[tap]
            parts = [whole[:cols] + halo[2 * tap][f], whole[cols : span - cols], whole[span - cols :] + halo[2 * tap + 1][f]]
            products[tap] = jnp.concatenate(parts, axis=0)
        conv = part_ref[here] + joined_columns(products, cols)
        mean = jnp.mean(conv * conv, axis=1, keepdims=True)
        normed = conv * lax.rsqrt(mean + 1e-06) * gain_ref[...]
        silu = 0.5 * normed * (1.0 + jnp.tanh(0.5 * normed))
        mine = jnp.concatenate(frame_rows(edge_ref, mid_ref, f), axis=0).astype(F32)
        feature_ref[here] = (mine + silu).astype(BF16)
    features = feature_ref[...]
    both = jnp.concatenate([features, target_ref[...]], axis=1)
    sums = jnp.dot(features.T, both, preferred_element_type=F32)
    cut = half // 2
    low = [sums[:half, :half], sums[:half, half:chans], sums[half : half + cut, half:chans]]
    high = [sums[:half, chans:], sums[half:, chans:], sums[half + cut :, half:chans]]
    low, high = jnp.concatenate(low, axis=0), jnp.concatenate(high, axis=0)

    @pl.when(even)
    def _():
        keep_ref[...] = low
        send_ref[...] = high

    @pl.when(jnp.logical_not(even))
    def _():
        keep_ref[...] = high
        send_ref[...] = low


def unpack_kernel(count, mine_ref, other_ref, gram_ref, cross_ref):
    half = mine_ref.shape[1]
    cut = half // 2

    def fill(low, high):
        corner = low[half : 2 * half] / count
        gram_ref[:half, :half] = low[:half] / count
        gram_ref[:half, half:] = corner
        gram_ref[half:, :half] = corner.T
        gram_ref[half : half + cut, half:] = low[2 * half :] / count
        gram_ref[half + cut :, half:] = high[2 * half :] / count
        cross_ref[...] = high[: 2 * half] / count

    @pl.when(on_even_row())
    def _():
        fill(mine_ref, other_ref)

    @pl.when(jnp.logical_not(on_even_row()))
    def _():
        fill(other_ref, mine_ref)


def places(mesh_axes=("tm", "row")):
    blocks, rows = (lax.axis_size(axis) for axis in mesh_axes)
    return [(a, b) for a in range(blocks) for b in range(rows)]


def with_mate(value):
    return by_device(value, [((a, b), (a, b ^ 1)) for a, b in places()])


def pack_kernel(keep_ref, got_ref, scaled_ref):
    rows, lanes = keep_ref.shape
    cut = 4 * rows // 5
    heads = []
    for here in (slice(0, cut), slice(cut, rows)):
        value = keep_ref[here] + got_ref[here]
        most = jnp.max(jnp.max(jnp.abs(value), axis=0, keepdims=True), axis=1, keepdims=True)
        exponent = jnp.floor(jnp.log2(jnp.maximum(most, 1e-30))) - 12.0
        scaled_ref[here] = value * jnp.exp2(-exponent)
        heads.append(jnp.broadcast_to(exponent, (HEAD // 2, lanes)))
    scaled_ref[rows:] = jnp.concatenate(heads, axis=0)


def power(exponent):
    return lax.reduce_precision(jnp.exp2(exponent), 8, 7)


def joined_messages(x, y, last):
    rows = x.shape[0] - HEAD
    cut = 4 * rows // 5
    x, y = x.astype(F32), y.astype(F32)
    row = lax.broadcasted_iota(jnp.int32, x.shape, 0)
    first = (row < cut) | ((row >= rows) & (row < rows + HEAD // 2))

    def spread(message):
        return jnp.where(first, message[rows : rows + 1], message[rows + HEAD // 2 : rows + HEAD // 2 + 1])

    p, q = spread(x), spread(y)
    if last:
        return (x * power(p) + y * power(q))[:rows]
    e = jnp.maximum(p, q) + 1.0
    return jnp.where(row < rows, x * power(p - e) + y * power(q - e), e).astype(F16)


def total_over_chips(keep, got):
    blocks, rows = lax.axis_size("tm"), lax.axis_size("row")
    steps = [("row", 2**k) for k in range(1, rows.bit_length() - 1)]
    steps += [("tm", 2**k) for k in range(blocks.bit_length() - 1)]
    size, lanes = keep.shape
    value = pl.pallas_call(
        pack_kernel,
        out_shape=jax.ShapeDtypeStruct((size + HEAD, lanes), F32),
        in_specs=[WHOLE] * 2,
        out_specs=WHOLE,
        compiler_params=params(4),
    )(keep, got).astype(F16)
    for s in range(len(steps)):
        value = lax.optimization_barrier(value)
        moves = []
        for a, b in places():
            swap = s ^ (b % 2)
            axis, bit = steps[swap if swap < len(steps) else s]
            moves.append(((a, b), (a ^ bit, b) if axis == "tm" else (a, b ^ bit)))
        value = joined_messages(value, by_device(value, moves), s == len(steps) - 1)
    return value


def on_device(latents, conv_weight, norm_gain, depth_target):
    frames, rows, cols, chans = latents.shape
    spots = frames * rows * cols
    bins = depth_target.shape[3]
    half = chans // 2
    blocks, bands = lax.axis_size("tm"), lax.axis_size("row")
    edge = jnp.stack([latents[:, 0], latents[:, -1]], axis=1)
    mid = latents[:, 1:-1]
    edge, mid = lax.optimization_barrier((edge, mid))
    old_edge = later(edge)
    old_mid = later(mid)
    rim = jax.ShapeDtypeStruct((2 * frames, cols, chans), BF16)
    mate, cross = pl.pallas_call(
        pick_kernel,
        out_shape=(rim, rim),
        in_specs=[WHOLE] * 2,
        out_specs=(WHOLE,) * 2,
        compiler_params=params(4),
        cost_estimate=pl.CostEstimate(flops=4 * 10**9, bytes_accessed=2**20, transcendentals=0),
    )(old_edge, edge)
    mate_rim = with_mate(mate)
    pairs = [((a, b), (a, ((b + 1) ^ 1) - 1)) for a, b in places() if 0 < b < bands - 1]
    cross_rim = by_device(cross, pairs)
    part = pl.pallas_call(
        own_kernel,
        out_shape=jax.ShapeDtypeStruct((spots, chans), F32),
        in_specs=[WHOLE] * 3,
        out_specs=WHOLE,
        compiler_params=params(24),
        cost_estimate=pl.CostEstimate(flops=spots * chans * chans * 27, bytes_accessed=5 * 2**20, transcendentals=0),
    )(edge, mid, conv_weight)
    features, keep, send = pl.pallas_call(
        rest_kernel,
        out_shape=(
            jax.ShapeDtypeStruct((spots, chans), BF16),
            jax.ShapeDtypeStruct((5 * half // 2, half), F32),
            jax.ShapeDtypeStruct((5 * half // 2, half), F32),
        ),
        in_specs=[WHOLE] * 10,
        out_specs=(WHOLE,) * 3,
        compiler_params=params(32),
        cost_estimate=pl.CostEstimate(flops=spots * chans * chans * 30, bytes_accessed=5 * 2**20, transcendentals=spots * chans),
    )(edge, mid, old_edge, old_mid, mate_rim, cross_rim, conv_weight, part,
      norm_gain.reshape(1, chans), depth_target.reshape(spots, bins))
    mine = total_over_chips(keep, with_mate(send))
    other = with_mate(mine)
    gram, cross = pl.pallas_call(
        functools.partial(unpack_kernel, spots * blocks * bands),
        out_shape=(jax.ShapeDtypeStruct((chans, chans), F32), jax.ShapeDtypeStruct((chans, bins), F32)),
        in_specs=[WHOLE] * 2,
        out_specs=(WHOLE,) * 2,
        compiler_params=params(4),
    )(mine, other)
    return features.reshape(latents.shape), gram, cross


def solution(mesh):
    in_specs = (P("tm", "row", None, None), P(), P(), P("tm", "row", None, None))
    out_specs = (P("tm", "row", None, None), P(), P())
    return jax.shard_map(
        on_device, mesh=mesh, in_specs=in_specs, out_specs=out_specs, check_vma=False
    )
```

```python
import functools

import jax
import jax.numpy as jnp
from jax import lax
from jax.experimental import pallas as pl
from jax.experimental.pallas import tpu as pltpu
from jax.sharding import PartitionSpec as P

F32 = jnp.float32
BF16 = jnp.bfloat16
F16 = jnp.float16
HEAD = 16
WHOLE = pl.BlockSpec(memory_space=pltpu.VMEM)


def params(mebibytes):
    return pltpu.CompilerParams(vmem_limit_bytes=mebibytes * 2**20)


def on_even_row():
    return lax.axis_index("row") % 2 == 0


def by_device(value, moves):
    rows = lax.axis_size("row")
    return lax.ppermute(value, ("tm", "row"), [(a * rows + b, c * rows + d) for (a, b), (c, d) in moves])


def later(value):
    count = lax.axis_size("tm")
    return lax.ppermute(value, "tm", [(i, (i + 1) % count) for i in range(count)])


def cut_kernel(latents_ref, edge_ref, mid_ref, mate_ref, cross_ref):
    last = latents_ref.shape[1] - 1
    edge_ref[:, 0] = latents_ref[:, 0]
    edge_ref[:, 1] = latents_ref[:, last]
    mid_ref[...] = latents_ref[:, 1:last]
    pick_kernel(edge_ref, mate_ref, cross_ref)


def pick_kernel(edge_ref, mate_ref, cross_ref):
    def fill(to_mate, to_cross):
        mate_ref[...] = edge_ref[:, to_mate]
        cross_ref[...] = edge_ref[:, to_cross]

    @pl.when(on_even_row())
    def _():
        fill(1, 0)

    @pl.when(jnp.logical_not(on_even_row()))
    def _():
        fill(0, 1)


def with_neighbour(value):
    bands = lax.axis_size("row")
    return by_device(value, [((a, b), (a, ((b + 1) ^ 1) - 1)) for a, b in places() if 0 < b < bands - 1])


def rims(mate_ref, cross_ref, f):
    even = on_even_row()
    mate, cross = mate_ref[f], cross_ref[f]
    return jnp.where(even, cross, mate), jnp.where(even, mate, cross)


def frame_rows(edge_ref, mid_ref, f):
    rows, cols, chans = mid_ref.shape[1:]
    return [edge_ref[f, 0], mid_ref[f].reshape(rows * cols, chans), edge_ref[f, 1]]


def column_taps(stacks, weight_ref, times, chans):
    rows = jnp.concatenate(stacks, axis=1)
    products = []
    for tap in range(3):
        weights = [weight_ref[t, dh, tap * chans : (tap + 1) * chans] for t in times for dh in range(3)]
        products.append(jnp.dot(rows, jnp.concatenate(weights, axis=0), preferred_element_type=F32))
    return products


def stacked_rows(rows, cols):
    wide = jnp.concatenate(rows, axis=0)
    span = wide.shape[0] - 2 * cols
    return jnp.concatenate([wide[tap * cols : tap * cols + span] for tap in range(3)], axis=1)


def joined_columns(products, cols):
    left, middle, right = products
    span = left.shape[0]
    col = lax.broadcasted_iota(jnp.int32, (span, 1), 0) % cols
    left = jnp.where(col == 0, 0.0, pltpu.roll(left, 1, 0))
    right = jnp.where(col == cols - 1, 0.0, pltpu.roll(right, span - 1, 0))
    return left + middle + right


def padded_stacks(edge_ref, mid_ref, mate_ref, cross_ref):
    cols = edge_ref.shape[2]
    stacks = []
    for f in range(2):
        above, below = rims(mate_ref, cross_ref, f)
        stacks.append(stacked_rows([above, *frame_rows(edge_ref, mid_ref, f), below], cols))
    return stacks


def own_kernel(edge_ref, mid_ref, mate_ref, cross_ref, weight_ref, part_ref):
    cols, chans = edge_ref.shape[2:]
    span = part_ref.shape[0] // 2
    stacks = padded_stacks(edge_ref, mid_ref, mate_ref, cross_ref)
    part_ref[:span] = joined_columns(column_taps(stacks[:1], weight_ref, [2], chans), cols)
    part_ref[span:] = joined_columns(column_taps(stacks, weight_ref, [1, 2], chans), cols)


def rest_kernel(edge_ref, mid_ref, old_edge_ref, old_mid_ref, mate_ref, cross_ref, weight_ref, part_ref,
                gain_ref, target_ref, feature_ref, keep_ref, send_ref):
    cols, chans = edge_ref.shape[2:]
    span, half = part_ref.shape[0] // 2, chans // 2
    stacks = padded_stacks(old_edge_ref, old_mid_ref, mate_ref, cross_ref)
    sums = jnp.zeros((chans, chans + target_ref.shape[1]), F32)
    for f in (1, 0):
        here = slice(f * span, (f + 1) * span)
        times = [0, 1] if f == 0 else [0]
        older = joined_columns(column_taps(stacks[f:], weight_ref, times, chans), cols)
        conv = part_ref[here] + jnp.where(lax.axis_index("tm") == 0, 0.0, older)
        mean = jnp.mean(conv * conv, axis=1, keepdims=True)
        normed = conv * lax.rsqrt(mean + 1e-06) * gain_ref[...]
        silu = 0.5 * normed * (1.0 + jnp.tanh(0.5 * normed))
        mine = jnp.concatenate(frame_rows(edge_ref, mid_ref, f), axis=0).astype(F32)
        features = (mine + silu).astype(BF16)
        feature_ref[here] = features
        both = jnp.concatenate([features, target_ref[here]], axis=1)
        sums = sums + jnp.dot(features.T, both, preferred_element_type=F32)
    row = lax.broadcasted_iota(jnp.int32, (half, half), 0)
    col = lax.broadcasted_iota(jnp.int32, (half, half), 1)
    head, tail = sums[:half, :half], sums[half:, half:chans]
    diagonal = jnp.sum(jnp.where(row == col, tail, 0.0), axis=0, keepdims=True)
    extra = jnp.concatenate([diagonal, jnp.zeros((HEAD // 2 - 1, half), F32)], axis=0)
    low = jnp.concatenate([jnp.where(row <= col, head, tail), sums[:half, half:chans], extra], axis=0)
    high = jnp.concatenate([sums[:half, chans:], sums[half:, chans:], jnp.zeros_like(extra)], axis=0)

    @pl.when(on_even_row())
    def _():
        keep_ref[...] = low
        send_ref[...] = high

    @pl.when(jnp.logical_not(on_even_row()))
    def _():
        keep_ref[...] = high
        send_ref[...] = low


def unpack_kernel(count, mine_ref, other_ref, gram_ref, cross_ref):
    half = mine_ref.shape[1]
    row = lax.broadcasted_iota(jnp.int32, (half, half), 0)
    col = lax.broadcasted_iota(jnp.int32, (half, half), 1)

    def fill(low, high):
        mixed, corner = low[:half] / count, low[half : 2 * half] / count
        diagonal = low[2 * half : 2 * half + 1] / count
        flipped = mixed.T
        gram_ref[:half, :half] = jnp.where(row <= col, mixed, flipped)
        gram_ref[:half, half:] = corner
        gram_ref[half:, :half] = corner.T
        gram_ref[half:, half:] = jnp.where(row > col, mixed, jnp.where(row == col, diagonal, flipped))
        cross_ref[...] = high[: 2 * half] / count

    @pl.when(on_even_row())
    def _():
        fill(mine_ref, other_ref)

    @pl.when(jnp.logical_not(on_even_row()))
    def _():
        fill(other_ref, mine_ref)


def places(mesh_axes=("tm", "row")):
    blocks, rows = (lax.axis_size(axis) for axis in mesh_axes)
    return [(a, b) for a in range(blocks) for b in range(rows)]


def with_mate(value):
    return by_device(value, [((a, b), (a, b ^ 1)) for a, b in places()])


def pack_kernel(keep_ref, got_ref, scaled_ref):
    rows, lanes = keep_ref.shape
    value = keep_ref[...] + got_ref[...]
    most = jnp.max(jnp.max(jnp.abs(value), axis=0, keepdims=True), axis=1, keepdims=True)
    exponent = jnp.floor(jnp.log2(jnp.maximum(most, 1e-30))) - 12.0
    scaled_ref[:rows] = value * jnp.exp2(-exponent)
    scaled_ref[rows:] = jnp.broadcast_to(exponent, (HEAD // 2, lanes))


def power(exponent):
    return lax.reduce_precision(jnp.exp2(exponent), 8, 7)


def joined_messages(messages, last):
    rows = messages[0].shape[0] - HEAD // 2
    messages = [message.astype(F32) for message in messages]
    exponents = [message[rows : rows + 1] for message in messages]
    e = functools.reduce(jnp.maximum, exponents) + len(messages) // 2
    if last:
        terms = [message[:rows] * power(p) for message, p in zip(messages, exponents)]
    else:
        terms = [message * power(p - e) for message, p in zip(messages, exponents)]
    while len(terms) > 1:
        terms = [a + b for a, b in zip(terms[::2], terms[1::2])]
    if last:
        return terms[0]
    row = lax.broadcasted_iota(jnp.int32, terms[0].shape, 0)
    return jnp.where(row < rows, terms[0], e).astype(F16)


def total_over_chips(keep, got):
    blocks, rows = lax.axis_size("tm"), lax.axis_size("row")
    bits = [(0, 2**k) for k in range(1, rows.bit_length() - 1)]
    bits += [(2**k, 0) for k in range(blocks.bit_length() - 1)]
    rounds = []
    for i in range(0, len(bits), 2):
        flips = bits[i : i + 2]
        if len(flips) == 2:
            flips.append((flips[0][0] ^ flips[1][0], flips[0][1] ^ flips[1][1]))
        rounds.append(flips)
    size, lanes = keep.shape
    value = pl.pallas_call(
        pack_kernel,
        out_shape=jax.ShapeDtypeStruct((size + HEAD // 2, lanes), F32),
        in_specs=[WHOLE] * 2,
        out_specs=WHOLE,
        compiler_params=params(4),
    )(keep, got).astype(F16)
    for s, flips in enumerate(rounds):
        value = lax.optimization_barrier(value)
        other = rounds[s ^ 1] if s ^ 1 < len(rounds) and len(rounds[s ^ 1]) == len(flips) else flips
        messages = [value]
        for pair in zip(flips, other):
            moves = [((a, b), (a ^ pair[b % 2][0], b ^ pair[b % 2][1])) for a, b in places()]
            messages.append(by_device(value, moves))
        value = joined_messages(messages, s == len(rounds) - 1)
    return value


def on_device(latents, conv_weight, norm_gain, depth_target):
    frames, rows, cols, chans = latents.shape
    spots = frames * rows * cols
    bins = depth_target.shape[3]
    half = chans // 2
    blocks, bands = lax.axis_size("tm"), lax.axis_size("row")
    rim = jax.ShapeDtypeStruct((frames, cols, chans), BF16)
    edge, mid, to_mate, to_cross = pl.pallas_call(
        cut_kernel,
        out_shape=(
            jax.ShapeDtypeStruct((frames, 2, cols, chans), BF16),
            jax.ShapeDtypeStruct((frames, rows - 2, cols, chans), BF16),
            rim,
            rim,
        ),
        in_specs=[WHOLE],
        out_specs=(WHOLE,) * 4,
        compiler_params=params(4),
    )(latents)
    old_edge = later(edge)
    old_mid = later(mid)
    mate, cross = with_mate(to_mate), with_neighbour(to_cross)
    old_to_mate, old_to_cross = pl.pallas_call(
        pick_kernel,
        out_shape=(rim, rim),
        in_specs=[WHOLE],
        out_specs=(WHOLE,) * 2,
        compiler_params=params(4),
        cost_estimate=pl.CostEstimate(flops=4 * 10**9, bytes_accessed=2**20, transcendentals=0),
    )(old_edge)
    old_mate, old_cross = with_mate(old_to_mate), with_neighbour(old_to_cross)
    part = pl.pallas_call(
        own_kernel,
        out_shape=jax.ShapeDtypeStruct((spots, chans), F32),
        in_specs=[WHOLE] * 5,
        out_specs=WHOLE,
        compiler_params=params(24),
        cost_estimate=pl.CostEstimate(flops=spots * chans * chans * 27, bytes_accessed=5 * 2**20, transcendentals=0),
    )(edge, mid, mate, cross, conv_weight)
    features, keep, send = pl.pallas_call(
        rest_kernel,
        out_shape=(
            jax.ShapeDtypeStruct((spots, chans), BF16),
            jax.ShapeDtypeStruct((2 * half + HEAD // 2, half), F32),
            jax.ShapeDtypeStruct((2 * half + HEAD // 2, half), F32),
        ),
        in_specs=[WHOLE] * 10,
        out_specs=(WHOLE,) * 3,
        compiler_params=params(32),
        cost_estimate=pl.CostEstimate(flops=spots * chans * chans * 30, bytes_accessed=5 * 2**20, transcendentals=spots * chans),
    )(edge, mid, old_edge, old_mid, old_mate, old_cross, conv_weight, part,
      norm_gain.reshape(1, chans), depth_target.reshape(spots, bins))
    mine = total_over_chips(keep, with_mate(send))
    other = with_mate(mine)
    gram, cross = pl.pallas_call(
        functools.partial(unpack_kernel, spots * blocks * bands),
        out_shape=(jax.ShapeDtypeStruct((chans, chans), F32), jax.ShapeDtypeStruct((chans, bins), F32)),
        in_specs=[WHOLE] * 2,
        out_specs=(WHOLE,) * 2,
        compiler_params=params(4),
    )(mine, other)
    return features.reshape(latents.shape), gram, cross


def solution(mesh):
    in_specs = (P("tm", "row", None, None), P(), P(), P("tm", "row", None, None))
    out_specs = (P("tm", "row", None, None), P(), P())
    return jax.shard_map(
        on_device, mesh=mesh, in_specs=in_specs, out_specs=out_specs, check_vma=False
    )
```

```python
import functools

import jax
import jax.numpy as jnp
from jax import lax
from jax.experimental import pallas as pl
from jax.experimental.pallas import tpu as pltpu
from jax.sharding import PartitionSpec as P

F32 = jnp.float32
BF16 = jnp.bfloat16
F16 = jnp.float16
HEAD = 16
WHOLE = pl.BlockSpec(memory_space=pltpu.VMEM)
ANY = pl.BlockSpec(memory_space=pl.ANY)


def params(mebibytes):
    return pltpu.CompilerParams(vmem_limit_bytes=mebibytes * 2**20)


def on_even_row():
    return lax.axis_index("row") % 2 == 0


def odd_bits(value):
    for shift in (8, 4, 2, 1):
        value = value ^ (value >> shift)
    return value & 1


def has_low():
    return odd_bits(lax.axis_index("tm") ^ lax.axis_index("row")) == 0


def by_device(value, moves):
    rows = lax.axis_size("row")
    return lax.ppermute(value, ("tm", "row"), [(a * rows + b, c * rows + d) for (a, b), (c, d) in moves])


def later(value):
    count = lax.axis_size("tm")
    return lax.ppermute(value, "tm", [(i, (i + 1) % count) for i in range(count)])


def cut_kernel(latents_ref, edge_ref, early_ref, late_ref, mate_ref, cross_ref):
    last = latents_ref.shape[1] - 1
    edge_ref[:, 0] = latents_ref[:, 0]
    edge_ref[:, 1] = latents_ref[:, last]
    early_ref[...] = latents_ref[0, 1:last]
    late_ref[...] = latents_ref[1, 1:last]
    pick_kernel(edge_ref, mate_ref, cross_ref)


def pick_kernel(edge_ref, mate_ref, cross_ref):
    def fill(to_mate, to_cross):
        mate_ref[...] = edge_ref[:, to_mate]
        cross_ref[...] = edge_ref[:, to_cross]

    @pl.when(on_even_row())
    def _():
        fill(1, 0)

    @pl.when(jnp.logical_not(on_even_row()))
    def _():
        fill(0, 1)


def with_neighbour(value):
    bands = lax.axis_size("row")
    return by_device(value, [((a, b), (a, (((b + 1) ^ 1) - 1) % bands)) for a, b in places()])


def rims(mate_ref, cross_ref, f):
    even = on_even_row()
    band = lax.axis_index("row")
    at_end = (band == 0) | (band == lax.axis_size("row") - 1)
    mate, cross = mate_ref[f], cross_ref[f]
    cross = jnp.where(at_end, jnp.zeros_like(cross), cross)
    return jnp.where(even, cross, mate), jnp.where(even, mate, cross)


def frame_rows(edge_ref, middle_ref, f):
    rows, cols, chans = middle_ref.shape
    return [edge_ref[f, 0], middle_ref[...].reshape(rows * cols, chans), edge_ref[f, 1]]


def column_taps(stacks, weight_ref, times, chans):
    rows = jnp.concatenate(stacks, axis=1)
    products = []
    for tap in range(3):
        weights = [weight_ref[t, dh, tap * chans : (tap + 1) * chans] for t in times for dh in range(3)]
        products.append(jnp.dot(rows, jnp.concatenate(weights, axis=0), preferred_element_type=F32))
    return products


def stacked_rows(rows, cols):
    wide = jnp.concatenate(rows, axis=0)
    span = wide.shape[0] - 2 * cols
    return jnp.concatenate([wide[tap * cols : tap * cols + span] for tap in range(3)], axis=1)


def joined_columns(products, cols):
    left, middle, right = products
    span = left.shape[0]
    col = lax.broadcasted_iota(jnp.int32, (span, 1), 0) % cols
    left = jnp.where(col == 0, 0.0, pltpu.roll(left, 1, 0))
    right = jnp.where(col == cols - 1, 0.0, pltpu.roll(right, span - 1, 0))
    return left + middle + right


def padded_stack(edge_ref, middle_ref, mate_ref, cross_ref, f):
    above, below = rims(mate_ref, cross_ref, f)
    return stacked_rows([above, *frame_rows(edge_ref, middle_ref, f), below], edge_ref.shape[2])


def own_kernel(edge_ref, early_ref, late_ref, mate_ref, cross_ref, weight_ref, part_ref):
    cols, chans = edge_ref.shape[2:]
    span = part_ref.shape[0] // 2
    early = padded_stack(edge_ref, early_ref, mate_ref, cross_ref, 0)
    late = padded_stack(edge_ref, late_ref, mate_ref, cross_ref, 1)
    part_ref[:span] = joined_columns(column_taps([early], weight_ref, [2], chans), cols)
    part_ref[span:] = joined_columns(column_taps([early, late], weight_ref, [1, 2], chans), cols)


def older_terms(stack, weight_ref, time, cols, chans):
    terms = joined_columns(column_taps([stack], weight_ref, [time], chans), cols)
    return jnp.where(lax.axis_index("tm") == 0, 0.0, terms)


def features_of(conv, own_rows, gain_ref):
    mean = jnp.mean(conv * conv, axis=1, keepdims=True)
    normed = conv * lax.rsqrt(mean + 1e-06) * gain_ref[...]
    silu = 0.5 * normed * (1.0 + jnp.tanh(0.5 * normed))
    return (jnp.concatenate(own_rows, axis=0).astype(F32) + silu).astype(BF16)


def moments(features, targets):
    both = jnp.concatenate([features, targets], axis=1)
    return jnp.dot(features.T, both, preferred_element_type=F32)


def late_kernel(edge_ref, late_ref, old_edge_ref, old_late_ref, mate_ref, cross_ref, weight_ref, part_ref, gain_ref,
                target_ref, feature_ref, more_ref, sums_ref, stage, sem):
    cols, chans = edge_ref.shape[2:]
    span = part_ref.shape[0] // 2
    stack = padded_stack(old_edge_ref, old_late_ref, mate_ref, cross_ref, 1)
    conv = part_ref[span:] + older_terms(stack, weight_ref, 0, cols, chans)
    features = features_of(conv, frame_rows(edge_ref, late_ref, 1), gain_ref)
    stage[...] = features
    copy = pltpu.make_async_copy(stage, feature_ref.at[pl.ds(span, span)], sem)
    copy.start()
    more_ref[...] = part_ref[:span] + older_terms(stack, weight_ref, 1, cols, chans)
    sums_ref[...] = moments(features, target_ref[span:])
    copy.wait()


def early_kernel(edge_ref, early_ref, old_edge_ref, old_early_ref, mate_ref, cross_ref, weight_ref, more_ref, sums_ref,
                 gain_ref, target_ref, late_feature_ref, feature_ref, keep_ref, send_ref, stage, sem):
    cols, chans = edge_ref.shape[2:]
    span, half = more_ref.shape[0], chans // 2
    stack = padded_stack(old_edge_ref, old_early_ref, mate_ref, cross_ref, 0)
    conv = more_ref[...] + older_terms(stack, weight_ref, 0, cols, chans)
    features = features_of(conv, frame_rows(edge_ref, early_ref, 0), gain_ref)
    stage[...] = features
    copy = pltpu.make_async_copy(stage, feature_ref.at[pl.ds(0, span)], sem)
    copy.start()
    sums = sums_ref[...] + moments(features, target_ref[:span])
    row = lax.broadcasted_iota(jnp.int32, (half, half), 0)
    col = lax.broadcasted_iota(jnp.int32, (half, half), 1)
    head, tail = sums[:half, :half], sums[half:, half:chans]
    diagonal = jnp.sum(jnp.where(row == col, tail, 0.0), axis=0, keepdims=True)
    extra = jnp.concatenate([diagonal, jnp.zeros((HEAD // 2 - 1, half), F32)], axis=0)
    low = jnp.concatenate([jnp.where(row <= col, head, tail), sums[:half, half:chans], extra], axis=0)
    high = jnp.concatenate([sums[:half, chans:], sums[half:, chans:], jnp.zeros_like(extra)], axis=0)

    @pl.when(has_low())
    def _():
        keep_ref[...] = low
        send_ref[...] = high

    @pl.when(jnp.logical_not(has_low()))
    def _():
        keep_ref[...] = high
        send_ref[...] = low

    copy.wait()


def unpack_kernel(count, mine_ref, other_ref, gram_ref, cross_ref):
    half = mine_ref.shape[1]
    row = lax.broadcasted_iota(jnp.int32, (half, half), 0)
    col = lax.broadcasted_iota(jnp.int32, (half, half), 1)

    def fill(low, high):
        mixed, corner = low[:half] / count, low[half : 2 * half] / count
        diagonal = low[2 * half : 2 * half + 1] / count
        flipped = mixed.T
        gram_ref[:half, :half] = jnp.where(row <= col, mixed, flipped)
        gram_ref[:half, half:] = corner
        gram_ref[half:, :half] = corner.T
        gram_ref[half:, half:] = jnp.where(row > col, mixed, jnp.where(row == col, diagonal, flipped))
        cross_ref[...] = high[: 2 * half] / count

    @pl.when(has_low())
    def _():
        fill(mine_ref, other_ref)

    @pl.when(jnp.logical_not(has_low()))
    def _():
        fill(other_ref, mine_ref)


def places(mesh_axes=("tm", "row")):
    blocks, rows = (lax.axis_size(axis) for axis in mesh_axes)
    return [(a, b) for a in range(blocks) for b in range(rows)]


def with_mate(value):
    return by_device(value, [((a, b), (a, b ^ 1)) for a, b in places()])


def pack_kernel(keep_ref, got_ref, scaled_ref):
    rows, lanes = keep_ref.shape
    value = keep_ref[...] + got_ref[...]
    most = jnp.max(jnp.max(jnp.abs(value), axis=0, keepdims=True), axis=1, keepdims=True)
    exponent = jnp.floor(jnp.log2(jnp.maximum(most, 1e-30))) - 12.0
    scaled_ref[:rows] = value * jnp.exp2(-exponent)
    scaled_ref[rows:] = jnp.broadcast_to(exponent, (HEAD // 2, lanes))


def power(exponent):
    return lax.reduce_precision(jnp.exp2(exponent), 8, 7)


def joined_messages(messages, last):
    rows = messages[0].shape[0] - HEAD // 2
    messages = [message.astype(F32) for message in messages]
    exponents = [message[rows : rows + 1] for message in messages]
    e = functools.reduce(jnp.maximum, exponents) + len(messages) // 2
    if last:
        terms = [message[:rows] * power(p) for message, p in zip(messages, exponents)]
    else:
        terms = [message * power(p - e) for message, p in zip(messages, exponents)]
    while len(terms) > 1:
        terms = [a + b for a, b in zip(terms[::2], terms[1::2])]
    if last:
        return terms[0]
    row = lax.broadcasted_iota(jnp.int32, terms[0].shape, 0)
    return jnp.where(row < rows, terms[0], e).astype(F16)


def total_over_chips(keep, got):
    blocks, rows = lax.axis_size("tm"), lax.axis_size("row")
    bits = [(0, 2**k) for k in range(1, rows.bit_length() - 1)]
    bits += [(2**k, 0) for k in range(blocks.bit_length() - 1)]
    rounds = []
    for i in range(0, len(bits), 2):
        flips = bits[i : i + 2]
        if len(flips) == 2:
            flips.append((flips[0][0] ^ flips[1][0], flips[0][1] ^ flips[1][1]))
        rounds.append(flips)
    size, lanes = keep.shape
    value = pl.pallas_call(
        pack_kernel,
        out_shape=jax.ShapeDtypeStruct((size + HEAD // 2, lanes), F32),
        in_specs=[WHOLE] * 2,
        out_specs=WHOLE,
        compiler_params=params(4),
    )(keep, got).astype(F16)
    for s, flips in enumerate(rounds):
        value = lax.optimization_barrier(value)
        other = rounds[s ^ 1] if s ^ 1 < len(rounds) and len(rounds[s ^ 1]) == len(flips) else flips
        messages = [value]
        for pair in zip(flips, other):
            moves = []
            for a, b in places():
                c, d = pair[odd_bits(a ^ b)]
                moves.append(((a, b), (a ^ c, b ^ d ^ odd_bits(c ^ d))))
            messages.append(by_device(value, moves))
        value = joined_messages(messages, s == len(rounds) - 1)
    return value


def on_device(latents, conv_weight, norm_gain, depth_target):
    frames, rows, cols, chans = latents.shape
    spots = frames * rows * cols
    bins = depth_target.shape[3]
    half = chans // 2
    blocks, bands = lax.axis_size("tm"), lax.axis_size("row")
    rim = jax.ShapeDtypeStruct((frames, cols, chans), BF16)
    middle = jax.ShapeDtypeStruct((rows - 2, cols, chans), BF16)
    edge, early, late, to_mate, to_cross = pl.pallas_call(
        cut_kernel,
        out_shape=(jax.ShapeDtypeStruct((frames, 2, cols, chans), BF16), middle, middle, rim, rim),
        in_specs=[WHOLE],
        out_specs=(WHOLE,) * 5,
        compiler_params=params(4),
    )(latents)
    old_edge, old_late, old_early = later(edge), later(late), later(early)
    mate, cross = with_mate(to_mate), with_neighbour(to_cross)
    old_to_mate, old_to_cross = pl.pallas_call(
        pick_kernel,
        out_shape=(rim, rim),
        in_specs=[WHOLE],
        out_specs=(WHOLE,) * 2,
        compiler_params=params(4),
        cost_estimate=pl.CostEstimate(flops=2 * 10**9, bytes_accessed=2**20, transcendentals=0),
    )(old_edge)
    old_mate, old_cross = with_mate(old_to_mate), with_neighbour(old_to_cross)
    part = pl.pallas_call(
        own_kernel,
        out_shape=jax.ShapeDtypeStruct((spots, chans), F32),
        in_specs=[WHOLE] * 6,
        out_specs=WHOLE,
        compiler_params=params(24),
        cost_estimate=pl.CostEstimate(flops=spots * chans * chans * 27, bytes_accessed=5 * 2**20, transcendentals=0),
    )(edge, early, late, mate, cross, conv_weight)
    gain, targets = norm_gain.reshape(1, chans), depth_target.reshape(spots, bins)
    half_features = jax.ShapeDtypeStruct((spots, chans), BF16)
    staging = [pltpu.VMEM((spots // 2, chans), BF16), pltpu.SemaphoreType.DMA]
    features, more, sums = pl.pallas_call(
        late_kernel,
        out_shape=(
            half_features,
            jax.ShapeDtypeStruct((spots // 2, chans), F32),
            jax.ShapeDtypeStruct((chans, chans + bins), F32),
        ),
        in_specs=[WHOLE] * 10,
        out_specs=(ANY, WHOLE, WHOLE),
        scratch_shapes=staging,
        compiler_params=params(24),
        cost_estimate=pl.CostEstimate(flops=spots * chans * chans * 20, bytes_accessed=5 * 2**20, transcendentals=spots * chans // 2),
    )(edge, late, old_edge, old_late, old_mate, old_cross, conv_weight, part, gain, targets)
    share = jax.ShapeDtypeStruct((2 * half + HEAD // 2, half), F32)
    features, keep, send = pl.pallas_call(
        early_kernel,
        out_shape=(half_features, share, share),
        in_specs=[WHOLE] * 11 + [ANY],
        out_specs=(ANY, WHOLE, WHOLE),
        scratch_shapes=staging,
        input_output_aliases={11: 0},
        compiler_params=params(24),
        cost_estimate=pl.CostEstimate(flops=spots * chans * chans * 10, bytes_accessed=5 * 2**20, transcendentals=spots * chans // 2),
    )(edge, early, old_edge, old_early, old_mate, old_cross, conv_weight, more, sums, gain, targets, features)
    mine = total_over_chips(keep, with_mate(send))
    other = with_mate(mine)
    gram, cross = pl.pallas_call(
        functools.partial(unpack_kernel, spots * blocks * bands),
        out_shape=(jax.ShapeDtypeStruct((chans, chans), F32), jax.ShapeDtypeStruct((chans, bins), F32)),
        in_specs=[WHOLE] * 2,
        out_specs=(WHOLE,) * 2,
        compiler_params=params(4),
    )(mine, other)
    return features.reshape(latents.shape), gram, cross


def solution(mesh):
    in_specs = (P("tm", "row", None, None), P(), P(), P("tm", "row", None, None))
    out_specs = (P("tm", "row", None, None), P(), P())
    return jax.shard_map(
        on_device, mesh=mesh, in_specs=in_specs, out_specs=out_specs, check_vma=False
    )
```

```python
import functools

import jax
import jax.numpy as jnp
from jax import lax
from jax.experimental import pallas as pl
from jax.experimental.pallas import tpu as pltpu
from jax.sharding import PartitionSpec as P

F32 = jnp.float32
BF16 = jnp.bfloat16
F16 = jnp.float16
HEAD = 16
WHOLE = pl.BlockSpec(memory_space=pltpu.VMEM)


def params(mebibytes):
    return pltpu.CompilerParams(vmem_limit_bytes=mebibytes * 2**20)


def on_even_row():
    return lax.axis_index("row") % 2 == 0


def odd_bits(value):
    for shift in (8, 4, 2, 1):
        value = value ^ (value >> shift)
    return value & 1


def has_low():
    return odd_bits(lax.axis_index("tm") ^ lax.axis_index("row")) == 0


def by_device(value, moves):
    rows = lax.axis_size("row")
    return lax.ppermute(value, ("tm", "row"), [(a * rows + b, c * rows + d) for (a, b), (c, d) in moves])


def later(value):
    count = lax.axis_size("tm")
    return lax.ppermute(value, "tm", [(i, (i + 1) % count) for i in range(count)])


def cut_kernel(latents_ref, edge_ref, early_ref, late_ref, mate_ref, cross_ref):
    last = latents_ref.shape[1] - 1
    edge_ref[:, 0] = latents_ref[:, 0]
    edge_ref[:, 1] = latents_ref[:, last]
    early_ref[...] = latents_ref[0, 1:last]
    late_ref[...] = latents_ref[1, 1:last]
    pick_kernel(edge_ref, mate_ref, cross_ref)


def pick_kernel(edge_ref, mate_ref, cross_ref):
    def fill(to_mate, to_cross):
        mate_ref[...] = edge_ref[:, to_mate]
        cross_ref[...] = edge_ref[:, to_cross]

    @pl.when(on_even_row())
    def _():
        fill(1, 0)

    @pl.when(jnp.logical_not(on_even_row()))
    def _():
        fill(0, 1)


def with_neighbour(value):
    bands = lax.axis_size("row")
    return by_device(value, [((a, b), (a, (((b + 1) ^ 1) - 1) % bands)) for a, b in places()])


def rims(mate_ref, cross_ref, f):
    even = on_even_row()
    band = lax.axis_index("row")
    at_end = (band == 0) | (band == lax.axis_size("row") - 1)
    mate, cross = mate_ref[f], cross_ref[f]
    cross = jnp.where(at_end, jnp.zeros_like(cross), cross)
    return jnp.where(even, cross, mate), jnp.where(even, mate, cross)


def frame_rows(edge_ref, middle_ref, f):
    rows, cols, chans = middle_ref.shape
    return [edge_ref[f, 0], middle_ref[...].reshape(rows * cols, chans), edge_ref[f, 1]]


def column_taps(stacks, weight_ref, times, chans):
    rows = jnp.concatenate(stacks, axis=1)
    products = []
    for tap in range(3):
        weights = [weight_ref[t, dh, tap * chans : (tap + 1) * chans] for t in times for dh in range(3)]
        products.append(jnp.dot(rows, jnp.concatenate(weights, axis=0), preferred_element_type=F32))
    return products


def stacked_rows(rows, cols):
    wide = jnp.concatenate(rows, axis=0)
    span = wide.shape[0] - 2 * cols
    return jnp.concatenate([wide[tap * cols : tap * cols + span] for tap in range(3)], axis=1)


def joined_columns(products, cols):
    left, middle, right = products
    span = left.shape[0]
    col = lax.broadcasted_iota(jnp.int32, (span, 1), 0) % cols
    left = jnp.where(col == 0, 0.0, pltpu.roll(left, 1, 0))
    right = jnp.where(col == cols - 1, 0.0, pltpu.roll(right, span - 1, 0))
    return left + middle + right


def padded_stack(edge_ref, middle_ref, mate_ref, cross_ref, f):
    above, below = rims(mate_ref, cross_ref, f)
    return stacked_rows([above, *frame_rows(edge_ref, middle_ref, f), below], edge_ref.shape[2])


def own_kernel(edge_ref, early_ref, late_ref, mate_ref, cross_ref, weight_ref, part_ref):
    cols, chans = edge_ref.shape[2:]
    span = part_ref.shape[0] // 2
    early = padded_stack(edge_ref, early_ref, mate_ref, cross_ref, 0)
    late = padded_stack(edge_ref, late_ref, mate_ref, cross_ref, 1)
    part_ref[:span] = joined_columns(column_taps([early], weight_ref, [2], chans), cols)
    part_ref[span:] = joined_columns(column_taps([early, late], weight_ref, [1, 2], chans), cols)


def older_terms(stack, weight_ref, time, cols, chans):
    terms = joined_columns(column_taps([stack], weight_ref, [time], chans), cols)
    return jnp.where(lax.axis_index("tm") == 0, 0.0, terms)


def features_of(conv, own_rows, gain_ref):
    mean = jnp.mean(conv * conv, axis=1, keepdims=True)
    normed = conv * lax.rsqrt(mean + 1e-06) * gain_ref[...]
    silu = 0.5 * normed * (1.0 + jnp.tanh(0.5 * normed))
    return (jnp.concatenate(own_rows, axis=0).astype(F32) + silu).astype(BF16)


def moments(features, targets):
    both = jnp.concatenate([features, targets], axis=1)
    return jnp.dot(features.T, both, preferred_element_type=F32)


def late_kernel(edge_ref, late_ref, old_edge_ref, old_late_ref, mate_ref, cross_ref, weight_ref, part_ref, gain_ref,
                target_ref, feature_ref, more_ref, sums_ref):
    cols, chans = edge_ref.shape[2:]
    span = part_ref.shape[0] // 2
    stack = padded_stack(old_edge_ref, old_late_ref, mate_ref, cross_ref, 1)
    conv = part_ref[span:] + older_terms(stack, weight_ref, 0, cols, chans)
    features = features_of(conv, frame_rows(edge_ref, late_ref, 1), gain_ref)
    feature_ref[...] = features
    more_ref[...] = part_ref[:span] + older_terms(stack, weight_ref, 1, cols, chans)
    sums_ref[...] = moments(features, target_ref[span:])


def early_kernel(edge_ref, early_ref, old_edge_ref, old_early_ref, mate_ref, cross_ref, weight_ref, more_ref, sums_ref,
                 gain_ref, target_ref, feature_ref, keep_ref, send_ref):
    cols, chans = edge_ref.shape[2:]
    span, half = more_ref.shape[0], chans // 2
    stack = padded_stack(old_edge_ref, old_early_ref, mate_ref, cross_ref, 0)
    conv = more_ref[...] + older_terms(stack, weight_ref, 0, cols, chans)
    features = features_of(conv, frame_rows(edge_ref, early_ref, 0), gain_ref)
    feature_ref[...] = features
    sums = sums_ref[...] + moments(features, target_ref[:span])
    row = lax.broadcasted_iota(jnp.int32, (half, half), 0)
    col = lax.broadcasted_iota(jnp.int32, (half, half), 1)
    head, tail = sums[:half, :half], sums[half:, half:chans]
    diagonal = jnp.sum(jnp.where(row == col, tail, 0.0), axis=0, keepdims=True)
    extra = jnp.concatenate([diagonal, jnp.zeros((HEAD // 2 - 1, half), F32)], axis=0)
    low = jnp.concatenate([jnp.where(row <= col, head, tail), sums[:half, half:chans], extra], axis=0)
    high = jnp.concatenate([sums[:half, chans:], sums[half:, chans:], jnp.zeros_like(extra)], axis=0)

    @pl.when(has_low())
    def _():
        keep_ref[...] = low
        send_ref[...] = high

    @pl.when(jnp.logical_not(has_low()))
    def _():
        keep_ref[...] = high
        send_ref[...] = low


def unpack_kernel(count, mine_ref, other_ref, gram_ref, cross_ref):
    half = mine_ref.shape[1]
    row = lax.broadcasted_iota(jnp.int32, (half, half), 0)
    col = lax.broadcasted_iota(jnp.int32, (half, half), 1)

    def fill(low, high):
        mixed, corner = low[:half] / count, low[half : 2 * half] / count
        diagonal = low[2 * half : 2 * half + 1] / count
        flipped = mixed.T
        gram_ref[:half, :half] = jnp.where(row <= col, mixed, flipped)
        gram_ref[:half, half:] = corner
        gram_ref[half:, :half] = corner.T
        gram_ref[half:, half:] = jnp.where(row > col, mixed, jnp.where(row == col, diagonal, flipped))
        cross_ref[...] = high[: 2 * half] / count

    @pl.when(has_low())
    def _():
        fill(mine_ref, other_ref)

    @pl.when(jnp.logical_not(has_low()))
    def _():
        fill(other_ref, mine_ref)


def places(mesh_axes=("tm", "row")):
    blocks, rows = (lax.axis_size(axis) for axis in mesh_axes)
    return [(a, b) for a in range(blocks) for b in range(rows)]


def with_mate(value):
    return by_device(value, [((a, b), (a, b ^ 1)) for a, b in places()])


def pack_kernel(keep_ref, got_ref, scaled_ref):
    rows, lanes = keep_ref.shape
    value = keep_ref[...] + got_ref[...]
    most = jnp.max(jnp.max(jnp.abs(value), axis=0, keepdims=True), axis=1, keepdims=True)
    exponent = jnp.floor(jnp.log2(jnp.maximum(most, 1e-30))) - 12.0
    scaled_ref[:rows] = value * jnp.exp2(-exponent)
    scaled_ref[rows:] = jnp.broadcast_to(exponent, (HEAD // 2, lanes))


def power(exponent):
    return lax.reduce_precision(jnp.exp2(exponent), 8, 7)


def joined_messages(messages, last):
    rows = messages[0].shape[0] - HEAD // 2
    messages = [message.astype(F32) for message in messages]
    exponents = [message[rows : rows + 1] for message in messages]
    e = functools.reduce(jnp.maximum, exponents) + len(messages) // 2
    if last:
        terms = [message[:rows] * power(p) for message, p in zip(messages, exponents)]
    else:
        terms = [message * power(p - e) for message, p in zip(messages, exponents)]
    while len(terms) > 1:
        terms = [a + b for a, b in zip(terms[::2], terms[1::2])]
    if last:
        return terms[0]
    row = lax.broadcasted_iota(jnp.int32, terms[0].shape, 0)
    return jnp.where(row < rows, terms[0], e).astype(F16)


def total_over_chips(keep, got):
    blocks, rows = lax.axis_size("tm"), lax.axis_size("row")
    bits = [(0, 2**k) for k in range(1, rows.bit_length() - 1)]
    bits += [(2**k, 0) for k in range(blocks.bit_length() - 1)]
    rounds = []
    for i in range(0, len(bits), 2):
        flips = bits[i : i + 2]
        if len(flips) == 2:
            flips.append((flips[0][0] ^ flips[1][0], flips[0][1] ^ flips[1][1]))
        rounds.append(flips)
    size, lanes = keep.shape
    value = pl.pallas_call(
        pack_kernel,
        out_shape=jax.ShapeDtypeStruct((size + HEAD // 2, lanes), F32),
        in_specs=[WHOLE] * 2,
        out_specs=WHOLE,
        compiler_params=params(4),
    )(keep, got).astype(F16)
    for s, flips in enumerate(rounds):
        value = lax.optimization_barrier(value)
        other = rounds[s ^ 1] if s ^ 1 < len(rounds) and len(rounds[s ^ 1]) == len(flips) else flips
        messages = [value]
        for pair in zip(flips, other):
            moves = []
            for a, b in places():
                c, d = pair[odd_bits(a ^ b)]
                moves.append(((a, b), (a ^ c, b ^ d ^ odd_bits(c ^ d))))
            messages.append(by_device(value, moves))
        value = joined_messages(messages[::-1], s == len(rounds) - 1)
    return value


def on_device(latents, conv_weight, norm_gain, depth_target):
    frames, rows, cols, chans = latents.shape
    spots = frames * rows * cols
    bins = depth_target.shape[3]
    half = chans // 2
    blocks, bands = lax.axis_size("tm"), lax.axis_size("row")
    rim = jax.ShapeDtypeStruct((frames, cols, chans), BF16)
    middle = jax.ShapeDtypeStruct((rows - 2, cols, chans), BF16)
    edge, early, late, to_mate, to_cross = pl.pallas_call(
        cut_kernel,
        out_shape=(jax.ShapeDtypeStruct((frames, 2, cols, chans), BF16), middle, middle, rim, rim),
        in_specs=[WHOLE],
        out_specs=(WHOLE,) * 5,
        compiler_params=params(4),
    )(latents)
    old_edge, old_late, old_early = later(edge), later(late), later(early)
    mate, cross = with_mate(to_mate), with_neighbour(to_cross)
    old_to_mate, old_to_cross = pl.pallas_call(
        pick_kernel,
        out_shape=(rim, rim),
        in_specs=[WHOLE],
        out_specs=(WHOLE,) * 2,
        compiler_params=params(4),
        cost_estimate=pl.CostEstimate(flops=2 * 10**9, bytes_accessed=2**20, transcendentals=0),
    )(old_edge)
    old_mate, old_cross = with_mate(old_to_mate), with_neighbour(old_to_cross)
    part = pl.pallas_call(
        own_kernel,
        out_shape=jax.ShapeDtypeStruct((spots, chans), F32),
        in_specs=[WHOLE] * 6,
        out_specs=WHOLE,
        compiler_params=params(24),
        cost_estimate=pl.CostEstimate(flops=spots * chans * chans * 27, bytes_accessed=5 * 2**20, transcendentals=0),
    )(edge, early, late, mate, cross, conv_weight)
    gain, targets = norm_gain.reshape(1, chans), depth_target.reshape(spots, bins)
    half_features = jax.ShapeDtypeStruct((spots // 2, chans), BF16)
    late_features, more, sums = pl.pallas_call(
        late_kernel,
        out_shape=(
            half_features,
            jax.ShapeDtypeStruct((spots // 2, chans), F32),
            jax.ShapeDtypeStruct((chans, chans + bins), F32),
        ),
        in_specs=[WHOLE] * 10,
        out_specs=(WHOLE,) * 3,
        compiler_params=params(24),
        cost_estimate=pl.CostEstimate(flops=spots * chans * chans * 20, bytes_accessed=5 * 2**20, transcendentals=spots * chans // 2),
    )(edge, late, old_edge, old_late, old_mate, old_cross, conv_weight, part, gain, targets)
    share = jax.ShapeDtypeStruct((2 * half + HEAD // 2, half), F32)
    early_features, keep, send = pl.pallas_call(
        early_kernel,
        out_shape=(half_features, share, share),
        in_specs=[WHOLE] * 11,
        out_specs=(WHOLE,) * 3,
        compiler_params=params(24),
        cost_estimate=pl.CostEstimate(flops=spots * chans * chans * 10, bytes_accessed=5 * 2**20, transcendentals=spots * chans // 2),
    )(edge, early, old_edge, old_early, old_mate, old_cross, conv_weight, more, sums, gain, targets)
    features = jnp.stack([early_features, late_features])
    mine = total_over_chips(keep, with_mate(send))
    mine, features = lax.optimization_barrier((mine, features))
    other = with_mate(mine)
    gram, cross = pl.pallas_call(
        functools.partial(unpack_kernel, spots * blocks * bands),
        out_shape=(jax.ShapeDtypeStruct((chans, chans), F32), jax.ShapeDtypeStruct((chans, bins), F32)),
        in_specs=[WHOLE] * 2,
        out_specs=(WHOLE,) * 2,
        compiler_params=params(4),
    )(mine, other)
    return features.reshape(latents.shape), gram, cross


def solution(mesh):
    in_specs = (P("tm", "row", None, None), P(), P(), P("tm", "row", None, None))
    out_specs = (P("tm", "row", None, None), P(), P())
    return jax.shard_map(
        on_device, mesh=mesh, in_specs=in_specs, out_specs=out_specs, check_vma=False
    )
```

```python
import functools

import jax
import jax.numpy as jnp
from jax import lax
from jax.experimental import pallas as pl
from jax.experimental.pallas import tpu as pltpu
from jax.sharding import PartitionSpec as P

F32 = jnp.float32
BF16 = jnp.bfloat16
F16 = jnp.float16
HEAD = 16
WHOLE = pl.BlockSpec(memory_space=pltpu.VMEM)


def params(mebibytes):
    return pltpu.CompilerParams(vmem_limit_bytes=mebibytes * 2**20)


def on_even_row():
    return lax.axis_index("row") % 2 == 0


def odd_bits(value):
    for shift in (8, 4, 2, 1):
        value = value ^ (value >> shift)
    return value & 1


def rounds_of_flips():
    blocks, rows = lax.axis_size("tm"), lax.axis_size("row")
    bits = [(0, 2**k) for k in range(1, rows.bit_length() - 1)]
    bits += [(2**k, 0) for k in range(blocks.bit_length() - 1)]
    rounds = []
    for i in range(0, len(bits), 2):
        flips = bits[i : i + 2]
        if len(flips) == 2:
            flips.append((flips[0][0] ^ flips[1][0], flips[0][1] ^ flips[1][1]))
        rounds.append(flips)
    return rounds


def side(a, b):
    counted = [flips[min(1, len(flips) - 1)] for flips in rounds_of_flips()]
    tm, row = sum(c for c, _ in counted), 1 + sum(d for _, d in counted)
    return odd_bits(a & tm) ^ odd_bits(b & row)


def has_low():
    return side(lax.axis_index("tm"), lax.axis_index("row")) == 0


def by_device(value, moves):
    rows = lax.axis_size("row")
    return lax.ppermute(value, ("tm", "row"), [(a * rows + b, c * rows + d) for (a, b), (c, d) in moves])


def later(value):
    count = lax.axis_size("tm")
    return lax.ppermute(value, "tm", [(i, (i + 1) % count) for i in range(count)])


def cut_kernel(latents_ref, edge_ref, early_ref, late_ref, mate_ref, cross_ref):
    last = latents_ref.shape[1] - 1
    edge_ref[:, 0] = latents_ref[:, 0]
    edge_ref[:, 1] = latents_ref[:, last]
    early_ref[...] = latents_ref[0, 1:last]
    late_ref[...] = latents_ref[1, 1:last]
    pick_kernel(edge_ref, mate_ref, cross_ref)


def pick_kernel(edge_ref, mate_ref, cross_ref):
    def fill(to_mate, to_cross):
        mate_ref[...] = edge_ref[:, to_mate]
        cross_ref[...] = edge_ref[:, to_cross]

    @pl.when(on_even_row())
    def _():
        fill(1, 0)

    @pl.when(jnp.logical_not(on_even_row()))
    def _():
        fill(0, 1)


def with_neighbour(value):
    bands = lax.axis_size("row")
    return by_device(value, [((a, b), (a, (((b + 1) ^ 1) - 1) % bands)) for a, b in places()])


def rims(mate_ref, cross_ref, f):
    even = on_even_row()
    band = lax.axis_index("row")
    at_end = (band == 0) | (band == lax.axis_size("row") - 1)
    mate, cross = mate_ref[f], cross_ref[f]
    cross = jnp.where(at_end, jnp.zeros_like(cross), cross)
    return jnp.where(even, cross, mate), jnp.where(even, mate, cross)


def frame_rows(edge_ref, middle_ref, f):
    rows, cols, chans = middle_ref.shape
    return [edge_ref[f, 0], middle_ref[...].reshape(rows * cols, chans), edge_ref[f, 1]]


def column_taps(stacks, weight_ref, times, chans):
    rows = jnp.concatenate(stacks, axis=1)
    products = []
    for tap in range(3):
        weights = [weight_ref[t, dh, tap * chans : (tap + 1) * chans] for t in times for dh in range(3)]
        products.append(jnp.dot(rows, jnp.concatenate(weights, axis=0), preferred_element_type=F32))
    return products


def stacked_rows(wide, start, span, cols):
    return jnp.concatenate([wide[start + tap * cols : start + tap * cols + span] for tap in range(3)], axis=1)


def joined_columns(products, cols):
    left, middle, right = products
    span = left.shape[0]
    col = lax.broadcasted_iota(jnp.int32, (span, 1), 0) % cols
    left = jnp.where(col == 0, 0.0, pltpu.roll(left, 1, 0))
    right = jnp.where(col == cols - 1, 0.0, pltpu.roll(right, span - 1, 0))
    return left + middle + right


def padded_frame(edge_ref, middle_ref, mate_ref, cross_ref, f):
    above, below = rims(mate_ref, cross_ref, f)
    return jnp.concatenate([above, *frame_rows(edge_ref, middle_ref, f), below], axis=0)


def own_kernel(edge_ref, early_ref, late_ref, mate_ref, cross_ref, weight_ref, part_ref):
    cols, chans = edge_ref.shape[2:]
    span = part_ref.shape[0] // 2
    early = stacked_rows(padded_frame(edge_ref, early_ref, mate_ref, cross_ref, 0), 0, span, cols)
    late = stacked_rows(padded_frame(edge_ref, late_ref, mate_ref, cross_ref, 1), 0, span, cols)
    part_ref[:span] = joined_columns(column_taps([early], weight_ref, [2], chans), cols)
    part_ref[span:] = joined_columns(column_taps([early, late], weight_ref, [1, 2], chans), cols)


def older_terms(wide, start, span, weight_ref, time, cols):
    stack = stacked_rows(wide, start, span, cols)
    terms = joined_columns(column_taps([stack], weight_ref, [time], wide.shape[1]), cols)
    return jnp.where(lax.axis_index("tm") == 0, 0.0, terms)


def chunks_of(span, cols):
    size = span // 2 if span % (2 * cols) == 0 else span
    return [(start, size) for start in range(0, span, size)]


def features_of(conv, own, gain_ref):
    mean = jnp.mean(conv * conv, axis=1, keepdims=True)
    normed = conv * lax.rsqrt(mean + 1e-06) * gain_ref[...]
    silu = 0.5 * normed * (1.0 + jnp.tanh(0.5 * normed))
    return (own.astype(F32) + silu).astype(BF16)


def moments(features, targets):
    both = jnp.concatenate([features, targets], axis=1)
    return jnp.dot(features.T, both, preferred_element_type=F32)


def late_kernel(edge_ref, late_ref, old_edge_ref, old_late_ref, cross_ref, mate_ref, weight_ref, part_ref, gain_ref,
                target_ref, feature_ref, more_ref, sums_ref):
    cols, chans = edge_ref.shape[2:]
    span = part_ref.shape[0] // 2
    wide = padded_frame(old_edge_ref, old_late_ref, mate_ref, cross_ref, 1)
    own = jnp.concatenate(frame_rows(edge_ref, late_ref, 1), axis=0)
    chunks = chunks_of(span, cols)
    older = [older_terms(wide, start, size, weight_ref, 0, cols) for start, size in chunks]
    more_ref[...] = part_ref[:span] + older_terms(wide, 0, span, weight_ref, 1, cols)
    sums = jnp.zeros(sums_ref.shape, F32)
    for (start, size), terms in zip(chunks, older):
        conv = part_ref[span + start : span + start + size] + terms
        features = features_of(conv, own[start : start + size], gain_ref)
        feature_ref[start : start + size] = features
        sums = sums + moments(features, target_ref[span + start : span + start + size])
    sums_ref[...] = sums


def early_kernel(edge_ref, early_ref, old_edge_ref, old_early_ref, cross_ref, mate_ref, weight_ref, more_ref, sums_ref,
                 gain_ref, target_ref, feature_ref, keep_ref, send_ref):
    cols, chans = edge_ref.shape[2:]
    span, half = more_ref.shape[0], chans // 2
    wide = padded_frame(old_edge_ref, old_early_ref, mate_ref, cross_ref, 0)
    own = jnp.concatenate(frame_rows(edge_ref, early_ref, 0), axis=0)
    chunks = chunks_of(span, cols)
    older = [older_terms(wide, start, size, weight_ref, 0, cols) for start, size in chunks]
    sums = sums_ref[...]
    for (start, size), terms in zip(chunks, older):
        features = features_of(more_ref[start : start + size] + terms, own[start : start + size], gain_ref)
        feature_ref[start : start + size] = features
        sums = sums + moments(features, target_ref[start : start + size])
    row = lax.broadcasted_iota(jnp.int32, (half, half), 0)
    col = lax.broadcasted_iota(jnp.int32, (half, half), 1)
    head, tail = sums[:half, :half], sums[half:, half:chans]
    diagonal = jnp.sum(jnp.where(row == col, tail, 0.0), axis=0, keepdims=True)
    extra = jnp.concatenate([diagonal, jnp.zeros((HEAD // 2 - 1, half), F32)], axis=0)
    low = jnp.concatenate([jnp.where(row <= col, head, tail), sums[:half, half:chans], extra], axis=0)
    high = jnp.concatenate([sums[:half, chans:], sums[half:, chans:], jnp.zeros_like(extra)], axis=0)

    @pl.when(has_low())
    def _():
        keep_ref[...] = low
        send_ref[...] = high

    @pl.when(jnp.logical_not(has_low()))
    def _():
        keep_ref[...] = high
        send_ref[...] = low


def unpack_kernel(count, mine_ref, other_ref, gram_ref, cross_ref):
    half = mine_ref.shape[1]
    row = lax.broadcasted_iota(jnp.int32, (half, half), 0)
    col = lax.broadcasted_iota(jnp.int32, (half, half), 1)

    def fill(low, high):
        mixed, corner = low[:half] / count, low[half : 2 * half] / count
        diagonal = low[2 * half : 2 * half + 1] / count
        flipped = mixed.T
        gram_ref[:half, :half] = jnp.where(row <= col, mixed, flipped)
        gram_ref[:half, half:] = corner
        gram_ref[half:, :half] = corner.T
        gram_ref[half:, half:] = jnp.where(row > col, mixed, jnp.where(row == col, diagonal, flipped))
        cross_ref[...] = high[: 2 * half] / count

    @pl.when(has_low())
    def _():
        fill(mine_ref, other_ref)

    @pl.when(jnp.logical_not(has_low()))
    def _():
        fill(other_ref, mine_ref)


def places(mesh_axes=("tm", "row")):
    blocks, rows = (lax.axis_size(axis) for axis in mesh_axes)
    return [(a, b) for a in range(blocks) for b in range(rows)]


def with_mate(value):
    return by_device(value, [((a, b), (a, b ^ 1)) for a, b in places()])


def pack_kernel(keep_ref, got_ref, scaled_ref):
    rows, lanes = keep_ref.shape
    value = keep_ref[...] + got_ref[...]
    most = jnp.max(jnp.max(jnp.abs(value), axis=0, keepdims=True), axis=1, keepdims=True)
    exponent = jnp.floor(jnp.log2(jnp.maximum(most, 1e-30))) - 12.0
    scaled_ref[:rows] = value * jnp.exp2(-exponent)
    scaled_ref[rows:] = jnp.broadcast_to(exponent, (HEAD // 2, lanes))


def power(exponent):
    return lax.reduce_precision(jnp.exp2(exponent), 8, 7)


def joined_messages(messages, last):
    rows = messages[0].shape[0] - HEAD // 2
    messages = [message.astype(F32) for message in messages]
    exponents = [message[rows : rows + 1] for message in messages]
    e = functools.reduce(jnp.maximum, exponents) + len(messages) // 2
    if last:
        terms = [message[:rows] * power(p) for message, p in zip(messages, exponents)]
    else:
        terms = [message * power(p - e) for message, p in zip(messages, exponents)]
    while len(terms) > 1:
        terms = [a + b for a, b in zip(terms[::2], terms[1::2])]
    if last:
        return terms[0]
    row = lax.broadcasted_iota(jnp.int32, terms[0].shape, 0)
    return jnp.where(row < rows, terms[0], e).astype(F16)


def total_over_chips(keep, got):
    rounds = rounds_of_flips()
    size, lanes = keep.shape
    value = pl.pallas_call(
        pack_kernel,
        out_shape=jax.ShapeDtypeStruct((size + HEAD // 2, lanes), F32),
        in_specs=[WHOLE] * 2,
        out_specs=WHOLE,
        compiler_params=params(4),
    )(keep, got).astype(F16)
    for s, flips in enumerate(rounds):
        value = lax.optimization_barrier(value)
        other = rounds[s ^ 1] if s ^ 1 < len(rounds) and len(rounds[s ^ 1]) == len(flips) else flips
        messages = [value]
        for pair in zip(flips, other):
            moves = []
            for a, b in places():
                c, d = pair[side(a, b)]
                moves.append(((a, b), (a ^ c, b ^ d ^ side(c, d))))
            messages.append(by_device(value, moves))
        value = joined_messages(messages[::-1], s == len(rounds) - 1)
    return value


def on_device(latents, conv_weight, norm_gain, depth_target):
    frames, rows, cols, chans = latents.shape
    spots = frames * rows * cols
    bins = depth_target.shape[3]
    half = chans // 2
    blocks, bands = lax.axis_size("tm"), lax.axis_size("row")
    rim = jax.ShapeDtypeStruct((frames, cols, chans), BF16)
    middle = jax.ShapeDtypeStruct((rows - 2, cols, chans), BF16)
    edge, early, late, to_mate, to_cross = pl.pallas_call(
        cut_kernel,
        out_shape=(jax.ShapeDtypeStruct((frames, 2, cols, chans), BF16), middle, middle, rim, rim),
        in_specs=[WHOLE],
        out_specs=(WHOLE,) * 5,
        compiler_params=params(4),
    )(latents)
    old_edge, old_late, old_early = later(edge), later(late), later(early)
    mate, cross = with_mate(to_mate), with_neighbour(to_cross)
    old_to_mate, old_to_cross = pl.pallas_call(
        pick_kernel,
        out_shape=(rim, rim),
        in_specs=[WHOLE],
        out_specs=(WHOLE,) * 2,
        compiler_params=params(4),
        cost_estimate=pl.CostEstimate(flops=2 * 10**9, bytes_accessed=2**20, transcendentals=0),
    )(old_edge)
    old_mate, old_cross = with_mate(old_to_mate), with_neighbour(old_to_cross)
    part = pl.pallas_call(
        own_kernel,
        out_shape=jax.ShapeDtypeStruct((spots, chans), F32),
        in_specs=[WHOLE] * 6,
        out_specs=WHOLE,
        compiler_params=params(24),
        cost_estimate=pl.CostEstimate(flops=spots * chans * chans * 27, bytes_accessed=5 * 2**20, transcendentals=0),
    )(edge, early, late, mate, cross, conv_weight)
    gain, targets = norm_gain.reshape(1, chans), depth_target.reshape(spots, bins)
    half_features = jax.ShapeDtypeStruct((spots // 2, chans), BF16)
    late_features, more, sums = pl.pallas_call(
        late_kernel,
        out_shape=(
            half_features,
            jax.ShapeDtypeStruct((spots // 2, chans), F32),
            jax.ShapeDtypeStruct((chans, chans + bins), F32),
        ),
        in_specs=[WHOLE] * 10,
        out_specs=(WHOLE,) * 3,
        compiler_params=params(24),
        cost_estimate=pl.CostEstimate(flops=spots * chans * chans * 20, bytes_accessed=5 * 2**20, transcendentals=spots * chans // 2),
    )(edge, late, old_edge, old_late, old_cross, old_mate, conv_weight, part, gain, targets)
    share = jax.ShapeDtypeStruct((2 * half + HEAD // 2, half), F32)
    early_features, keep, send = pl.pallas_call(
        early_kernel,
        out_shape=(half_features, share, share),
        in_specs=[WHOLE] * 11,
        out_specs=(WHOLE,) * 3,
        compiler_params=params(24),
        cost_estimate=pl.CostEstimate(flops=spots * chans * chans * 10, bytes_accessed=5 * 2**20, transcendentals=spots * chans // 2),
    )(edge, early, old_edge, old_early, old_cross, old_mate, conv_weight, more, sums, gain, targets)
    features = jnp.stack([early_features, late_features])
    mine = total_over_chips(keep, with_mate(send))
    mine, features = lax.optimization_barrier((mine, features))
    other = with_mate(mine)
    gram, cross = pl.pallas_call(
        functools.partial(unpack_kernel, spots * blocks * bands),
        out_shape=(jax.ShapeDtypeStruct((chans, chans), F32), jax.ShapeDtypeStruct((chans, bins), F32)),
        in_specs=[WHOLE] * 2,
        out_specs=(WHOLE,) * 2,
        compiler_params=params(4),
    )(mine, other)
    return features.reshape(latents.shape), gram, cross


def solution(mesh):
    in_specs = (P("tm", "row", None, None), P(), P(), P("tm", "row", None, None))
    out_specs = (P("tm", "row", None, None), P(), P())
    return jax.shard_map(
        on_device, mesh=mesh, in_specs=in_specs, out_specs=out_specs, check_vma=False
    )
```

```python
import functools

import jax
import jax.numpy as jnp
from jax import lax
from jax.experimental import pallas as pl
from jax.experimental.pallas import tpu as pltpu
from jax.sharding import PartitionSpec as P

F32 = jnp.float32
BF16 = jnp.bfloat16
F16 = jnp.float16
HEAD = 16
WHOLE = pl.BlockSpec(memory_space=pltpu.VMEM)


def params(mebibytes):
    return pltpu.CompilerParams(vmem_limit_bytes=mebibytes * 2**20)


def on_even_row():
    return lax.axis_index("row") % 2 == 0


def odd_bits(value):
    for shift in (8, 4, 2, 1):
        value = value ^ (value >> shift)
    return value & 1


def rounds_of_flips():
    blocks, rows = lax.axis_size("tm"), lax.axis_size("row")
    bits = [(0, 2**k) for k in range(1, rows.bit_length() - 1)]
    bits += [(2**k, 0) for k in range(blocks.bit_length() - 1)]
    rounds = []
    for i in range(0, len(bits), 2):
        flips = bits[i : i + 2]
        if len(flips) == 2:
            flips.append((flips[0][0] ^ flips[1][0], flips[0][1] ^ flips[1][1]))
        rounds.append(flips)
    return rounds


def side(a, b):
    counted = [flips[min(1, len(flips) - 1)] for flips in rounds_of_flips()]
    tm, row = sum(c for c, _ in counted), 1 + sum(d for _, d in counted)
    return odd_bits(a & tm) ^ odd_bits(b & row)


def has_low():
    return side(lax.axis_index("tm"), lax.axis_index("row")) == 0


def by_device(value, moves):
    rows = lax.axis_size("row")
    return lax.ppermute(value, ("tm", "row"), [(a * rows + b, c * rows + d) for (a, b), (c, d) in moves])


def later(value):
    count = lax.axis_size("tm")
    return lax.ppermute(value, "tm", [(i, (i + 1) % count) for i in range(count)])


def cut_kernel(latents_ref, edge_ref, early_ref, late_ref, mate_ref, cross_ref):
    last = latents_ref.shape[1] - 1
    early_ref[...] = latents_ref[0, 1:last]
    late_ref[...] = latents_ref[1, 1:last]
    pick_kernel(edge_ref, mate_ref, cross_ref)


def pick_kernel(edge_ref, mate_ref, cross_ref):
    def fill(to_mate, to_cross):
        mate_ref[...] = edge_ref[:, to_mate]
        cross_ref[...] = edge_ref[:, to_cross]

    @pl.when(on_even_row())
    def _():
        fill(1, 0)

    @pl.when(jnp.logical_not(on_even_row()))
    def _():
        fill(0, 1)


def with_neighbour(value):
    bands = lax.axis_size("row")
    return by_device(value, [((a, b), (a, (((b + 1) ^ 1) - 1) % bands)) for a, b in places()])


def rims(mate_ref, cross_ref, f):
    even = on_even_row()
    band = lax.axis_index("row")
    at_end = (band == 0) | (band == lax.axis_size("row") - 1)
    mate, cross = mate_ref[f], cross_ref[f]
    cross = jnp.where(at_end, jnp.zeros_like(cross), cross)
    return jnp.where(even, cross, mate), jnp.where(even, mate, cross)


def frame_rows(edge_ref, middle_ref, f):
    rows, cols, chans = middle_ref.shape
    return [edge_ref[f, 0], middle_ref[...].reshape(rows * cols, chans), edge_ref[f, 1]]


def column_taps(stacks, weight_ref, times, chans):
    rows = jnp.concatenate(stacks, axis=1)
    products = []
    for tap in range(3):
        weights = [weight_ref[t, dh, tap * chans : (tap + 1) * chans] for t in times for dh in range(3)]
        products.append(jnp.dot(rows, jnp.concatenate(weights, axis=0), preferred_element_type=F32))
    return products


def stacked_rows(wide, start, span, cols):
    return jnp.concatenate([wide[start + tap * cols : start + tap * cols + span] for tap in range(3)], axis=1)


def joined_columns(products, cols):
    left, middle, right = products
    span = left.shape[0]
    col = lax.broadcasted_iota(jnp.int32, (span, 1), 0) % cols
    left = jnp.where(col == 0, 0.0, pltpu.roll(left, 1, 0))
    right = jnp.where(col == cols - 1, 0.0, pltpu.roll(right, span - 1, 0))
    return left + middle + right


def padded_frame(edge_ref, middle_ref, mate_ref, cross_ref, f):
    above, below = rims(mate_ref, cross_ref, f)
    return jnp.concatenate([above, *frame_rows(edge_ref, middle_ref, f), below], axis=0)


def own_kernel(edge_ref, early_ref, late_ref, mate_ref, cross_ref, weight_ref, part_ref):
    cols, chans = edge_ref.shape[2:]
    span = part_ref.shape[0] // 2
    early = stacked_rows(padded_frame(edge_ref, early_ref, mate_ref, cross_ref, 0), 0, span, cols)
    late = stacked_rows(padded_frame(edge_ref, late_ref, mate_ref, cross_ref, 1), 0, span, cols)
    part_ref[:span] = joined_columns(column_taps([early], weight_ref, [2], chans), cols)
    part_ref[span:] = joined_columns(column_taps([early, late], weight_ref, [1, 2], chans), cols)


def older_terms(wide, start, span, weight_ref, time, cols):
    stack = stacked_rows(wide, start, span, cols)
    terms = joined_columns(column_taps([stack], weight_ref, [time], wide.shape[1]), cols)
    return jnp.where(lax.axis_index("tm") == 0, 0.0, terms)


def chunks_of(span, cols):
    size = span // 2 if span % (2 * cols) == 0 else span
    return [(start, size) for start in range(0, span, size)]


def features_of(conv, own, gain_ref):
    mean = jnp.mean(conv * conv, axis=1, keepdims=True)
    normed = conv * lax.rsqrt(mean + 1e-06) * gain_ref[...]
    silu = 0.5 * normed * (1.0 + jnp.tanh(0.5 * normed))
    return (own.astype(F32) + silu).astype(BF16)


def moments(features, targets):
    both = jnp.concatenate([features, targets], axis=1)
    return jnp.dot(features.T, both, preferred_element_type=F32)


def late_kernel(edge_ref, late_ref, old_edge_ref, old_late_ref, cross_ref, mate_ref, weight_ref, part_ref, gain_ref,
                target_ref, feature_ref, more_ref, sums_ref):
    cols, chans = edge_ref.shape[2:]
    span = part_ref.shape[0] // 2
    wide = padded_frame(old_edge_ref, old_late_ref, mate_ref, cross_ref, 1)
    own = jnp.concatenate(frame_rows(edge_ref, late_ref, 1), axis=0)
    chunks = chunks_of(span, cols)
    older = [older_terms(wide, start, size, weight_ref, 0, cols) for start, size in chunks]
    more_ref[...] = part_ref[:span] + older_terms(wide, 0, span, weight_ref, 1, cols)
    sums = jnp.zeros(sums_ref.shape, F32)
    for (start, size), terms in zip(chunks, older):
        conv = part_ref[span + start : span + start + size] + terms
        features = features_of(conv, own[start : start + size], gain_ref)
        feature_ref[start : start + size] = features
        sums = sums + moments(features, target_ref[span + start : span + start + size])
    sums_ref[...] = sums


def early_kernel(edge_ref, early_ref, old_edge_ref, old_early_ref, cross_ref, mate_ref, weight_ref, more_ref, sums_ref,
                 gain_ref, target_ref, feature_ref, keep_ref, send_ref):
    cols, chans = edge_ref.shape[2:]
    span, half = more_ref.shape[0], chans // 2
    wide = padded_frame(old_edge_ref, old_early_ref, mate_ref, cross_ref, 0)
    own = jnp.concatenate(frame_rows(edge_ref, early_ref, 0), axis=0)
    chunks = chunks_of(span, cols)
    older = [older_terms(wide, start, size, weight_ref, 0, cols) for start, size in chunks]
    sums = sums_ref[...]
    for (start, size), terms in zip(chunks, older):
        features = features_of(more_ref[start : start + size] + terms, own[start : start + size], gain_ref)
        feature_ref[start : start + size] = features
        sums = sums + moments(features, target_ref[start : start + size])
    row = lax.broadcasted_iota(jnp.int32, (half, half), 0)
    col = lax.broadcasted_iota(jnp.int32, (half, half), 1)
    head, tail = sums[:half, :half], sums[half:, half:chans]
    diagonal = jnp.sum(jnp.where(row == col, tail, 0.0), axis=0, keepdims=True)
    extra = jnp.concatenate([diagonal, jnp.zeros((HEAD // 2 - 1, half), F32)], axis=0)
    low = jnp.concatenate([jnp.where(row <= col, head, tail), sums[:half, half:chans], extra], axis=0)
    high = jnp.concatenate([sums[:half, chans:], sums[half:, chans:], jnp.zeros_like(extra)], axis=0)

    @pl.when(has_low())
    def _():
        keep_ref[...] = low
        send_ref[...] = high

    @pl.when(jnp.logical_not(has_low()))
    def _():
        keep_ref[...] = high
        send_ref[...] = low


def unpack_kernel(count, mine_ref, other_ref, gram_ref, cross_ref):
    half = mine_ref.shape[1]
    row = lax.broadcasted_iota(jnp.int32, (half, half), 0)
    col = lax.broadcasted_iota(jnp.int32, (half, half), 1)

    def fill(low, high):
        mixed, corner = low[:half] / count, low[half : 2 * half] / count
        diagonal = low[2 * half : 2 * half + 1] / count
        flipped = mixed.T
        gram_ref[:half, :half] = jnp.where(row <= col, mixed, flipped)
        gram_ref[:half, half:] = corner
        gram_ref[half:, :half] = corner.T
        gram_ref[half:, half:] = jnp.where(row > col, mixed, jnp.where(row == col, diagonal, flipped))
        cross_ref[...] = high[: 2 * half] / count

    @pl.when(has_low())
    def _():
        fill(mine_ref, other_ref)

    @pl.when(jnp.logical_not(has_low()))
    def _():
        fill(other_ref, mine_ref)


def places(mesh_axes=("tm", "row")):
    blocks, rows = (lax.axis_size(axis) for axis in mesh_axes)
    return [(a, b) for a in range(blocks) for b in range(rows)]


def with_mate(value):
    return by_device(value, [((a, b), (a, b ^ 1)) for a, b in places()])


def pack_kernel(keep_ref, got_ref, scaled_ref):
    rows, lanes = keep_ref.shape
    value = keep_ref[...] + got_ref[...]
    most = jnp.max(jnp.max(jnp.abs(value), axis=0, keepdims=True), axis=1, keepdims=True)
    exponent = jnp.floor(jnp.log2(jnp.maximum(most, 1e-30))) - 12.0
    scaled_ref[:rows] = value * jnp.exp2(-exponent)
    scaled_ref[rows:] = jnp.broadcast_to(exponent, (HEAD // 2, lanes))


def power(exponent):
    return lax.reduce_precision(jnp.exp2(exponent), 8, 7)


def joined_messages(messages, last):
    rows = messages[0].shape[0] - HEAD // 2
    messages = [message.astype(F32) for message in messages]
    exponents = [message[rows : rows + 1] for message in messages]
    e = functools.reduce(jnp.maximum, exponents) + len(messages) // 2
    if last:
        terms = [message[:rows] * power(p) for message, p in zip(messages, exponents)]
    else:
        terms = [message * power(p - e) for message, p in zip(messages, exponents)]
    while len(terms) > 1:
        terms = [a + b for a, b in zip(terms[::2], terms[1::2])]
    if last:
        return terms[0]
    row = lax.broadcasted_iota(jnp.int32, terms[0].shape, 0)
    return jnp.where(row < rows, terms[0], e).astype(F16)


def total_over_chips(keep, got):
    rounds = rounds_of_flips()
    size, lanes = keep.shape
    value = pl.pallas_call(
        pack_kernel,
        out_shape=jax.ShapeDtypeStruct((size + HEAD // 2, lanes), F32),
        in_specs=[WHOLE] * 2,
        out_specs=WHOLE,
        compiler_params=params(4),
    )(keep, got).astype(F16)
    for s, flips in enumerate(rounds):
        value = lax.optimization_barrier(value)
        other = rounds[s ^ 1] if s ^ 1 < len(rounds) and len(rounds[s ^ 1]) == len(flips) else flips
        messages = [value]
        for pair in zip(flips, other):
            moves = []
            for a, b in places():
                c, d = pair[side(a, b)]
                moves.append(((a, b), (a ^ c, b ^ d ^ side(c, d))))
            messages.append(by_device(value, moves))
        value = joined_messages(messages[::-1], s == len(rounds) - 1)
    return value


def on_device(latents, conv_weight, norm_gain, depth_target):
    frames, rows, cols, chans = latents.shape
    spots = frames * rows * cols
    bins = depth_target.shape[3]
    half = chans // 2
    blocks, bands = lax.axis_size("tm"), lax.axis_size("row")
    rim = jax.ShapeDtypeStruct((frames, cols, chans), BF16)
    middle = jax.ShapeDtypeStruct((rows - 2, cols, chans), BF16)
    edge = latents[:, :: rows - 1]
    early, late, to_mate, to_cross = pl.pallas_call(
        cut_kernel,
        out_shape=(middle, middle, rim, rim),
        in_specs=[WHOLE] * 2,
        out_specs=(WHOLE,) * 4,
        compiler_params=params(4),
    )(latents, edge)
    old_edge, old_late, old_early = later(edge), later(late), later(early)
    mate, cross = with_mate(to_mate), with_neighbour(to_cross)
    old_to_mate, old_to_cross = pl.pallas_call(
        pick_kernel,
        out_shape=(rim, rim),
        in_specs=[WHOLE],
        out_specs=(WHOLE,) * 2,
        compiler_params=params(4),
        cost_estimate=pl.CostEstimate(flops=2 * 10**9, bytes_accessed=2**20, transcendentals=0),
    )(old_edge)
    old_mate, old_cross = with_mate(old_to_mate), with_neighbour(old_to_cross)
    part = pl.pallas_call(
        own_kernel,
        out_shape=jax.ShapeDtypeStruct((spots, chans), F32),
        in_specs=[WHOLE] * 6,
        out_specs=WHOLE,
        compiler_params=params(24),
        cost_estimate=pl.CostEstimate(flops=spots * chans * chans * 27, bytes_accessed=5 * 2**20, transcendentals=0),
    )(edge, early, late, mate, cross, conv_weight)
    gain, targets = norm_gain.reshape(1, chans), depth_target.reshape(spots, bins)
    half_features = jax.ShapeDtypeStruct((spots // 2, chans), BF16)
    late_features, more, sums = pl.pallas_call(
        late_kernel,
        out_shape=(
            half_features,
            jax.ShapeDtypeStruct((spots // 2, chans), F32),
            jax.ShapeDtypeStruct((chans, chans + bins), F32),
        ),
        in_specs=[WHOLE] * 10,
        out_specs=(WHOLE,) * 3,
        compiler_params=params(24),
        cost_estimate=pl.CostEstimate(flops=spots * chans * chans * 20, bytes_accessed=5 * 2**20, transcendentals=spots * chans // 2),
    )(edge, late, old_edge, old_late, old_cross, old_mate, conv_weight, part, gain, targets)
    share = jax.ShapeDtypeStruct((2 * half + HEAD // 2, half), F32)
    early_features, keep, send = pl.pallas_call(
        early_kernel,
        out_shape=(half_features, share, share),
        in_specs=[WHOLE] * 11,
        out_specs=(WHOLE,) * 3,
        compiler_params=params(24),
        cost_estimate=pl.CostEstimate(flops=spots * chans * chans * 10, bytes_accessed=5 * 2**20, transcendentals=spots * chans // 2),
    )(edge, early, old_edge, old_early, old_cross, old_mate, conv_weight, more, sums, gain, targets)
    features = jnp.stack([early_features, late_features])
    mine = total_over_chips(keep, with_mate(send))
    mine, features = lax.optimization_barrier((mine, features))
    other = with_mate(mine)
    gram, cross = pl.pallas_call(
        functools.partial(unpack_kernel, spots * blocks * bands),
        out_shape=(jax.ShapeDtypeStruct((chans, chans), F32), jax.ShapeDtypeStruct((chans, bins), F32)),
        in_specs=[WHOLE] * 2,
        out_specs=(WHOLE,) * 2,
        compiler_params=params(4),
    )(mine, other)
    return features.reshape(latents.shape), gram, cross


def solution(mesh):
    in_specs = (P("tm", "row", None, None), P(), P(), P("tm", "row", None, None))
    out_specs = (P("tm", "row", None, None), P(), P())
    return jax.shard_map(
        on_device, mesh=mesh, in_specs=in_specs, out_specs=out_specs, check_vma=False
    )
```

```python
import functools

import jax
import jax.numpy as jnp
from jax import lax
from jax.experimental import pallas as pl
from jax.experimental.pallas import tpu as pltpu
from jax.sharding import PartitionSpec as P

F32 = jnp.float32
BF16 = jnp.bfloat16
F16 = jnp.float16
HEAD = 16
WHOLE = pl.BlockSpec(memory_space=pltpu.VMEM)


def params(mebibytes):
    return pltpu.CompilerParams(vmem_limit_bytes=mebibytes * 2**20)


def on_even_row():
    return lax.axis_index("row") % 2 == 0


def odd_bits(value):
    for shift in (8, 4, 2, 1):
        value = value ^ (value >> shift)
    return value & 1


def rounds_of_flips():
    blocks, rows = lax.axis_size("tm"), lax.axis_size("row")
    bits = [(0, 2**k) for k in range(1, rows.bit_length() - 1)]
    bits += [(2**k, 0) for k in range(blocks.bit_length() - 1)]
    rounds = []
    for i in range(0, len(bits), 2):
        flips = bits[i : i + 2]
        if len(flips) == 2:
            flips.append((flips[0][0] ^ flips[1][0], flips[0][1] ^ flips[1][1]))
        rounds.append(flips)
    return rounds


def side(a, b):
    counted = [flips[min(1, len(flips) - 1)] for flips in rounds_of_flips()]
    tm, row = sum(c for c, _ in counted), 1 + sum(d for _, d in counted)
    return odd_bits(a & tm) ^ odd_bits(b & row)


def has_low():
    return side(lax.axis_index("tm"), lax.axis_index("row")) == 0


def by_device(value, moves):
    rows = lax.axis_size("row")
    return lax.ppermute(value, ("tm", "row"), [(a * rows + b, c * rows + d) for (a, b), (c, d) in moves])


def later(value):
    count = lax.axis_size("tm")
    return lax.ppermute(value, "tm", [(i, (i + 1) % count) for i in range(count)])


def cut_kernel(latents_ref, edge_ref, early_ref, late_ref, mate_ref, cross_ref):
    last = latents_ref.shape[1] - 1
    early_ref[...] = latents_ref[0, 1:last]
    late_ref[...] = latents_ref[1, 1:last]
    pick_kernel(edge_ref, mate_ref, cross_ref)


def pick_kernel(edge_ref, mate_ref, cross_ref):
    def fill(to_mate, to_cross):
        mate_ref[...] = edge_ref[:, to_mate]
        cross_ref[...] = edge_ref[:, to_cross]

    @pl.when(on_even_row())
    def _():
        fill(1, 0)

    @pl.when(jnp.logical_not(on_even_row()))
    def _():
        fill(0, 1)


def with_neighbour(value):
    bands = lax.axis_size("row")
    return by_device(value, [((a, b), (a, (((b + 1) ^ 1) - 1) % bands)) for a, b in places()])


def rims(mate_ref, cross_ref, f):
    even = on_even_row()
    band = lax.axis_index("row")
    at_end = (band == 0) | (band == lax.axis_size("row") - 1)
    mate, cross = mate_ref[f], cross_ref[f]
    cross = jnp.where(at_end, jnp.zeros_like(cross), cross)
    return jnp.where(even, cross, mate), jnp.where(even, mate, cross)


def frame_rows(edge_ref, middle_ref, f):
    rows, cols, chans = middle_ref.shape
    return [edge_ref[f, 0], middle_ref[...].reshape(rows * cols, chans), edge_ref[f, 1]]


def column_taps(stacks, weight_ref, times, chans):
    rows = jnp.concatenate(stacks, axis=1)
    products = []
    for tap in range(3):
        weights = [weight_ref[t, dh, tap * chans : (tap + 1) * chans] for t in times for dh in range(3)]
        products.append(jnp.dot(rows, jnp.concatenate(weights, axis=0), preferred_element_type=F32))
    return products


def stacked_rows(wide, start, span, cols):
    return jnp.concatenate([wide[start + tap * cols : start + tap * cols + span] for tap in range(3)], axis=1)


def joined_columns(products, cols):
    left, middle, right = products
    span = left.shape[0]
    col = lax.broadcasted_iota(jnp.int32, (span, 1), 0) % cols
    left = jnp.where(col == 0, 0.0, pltpu.roll(left, 1, 0))
    right = jnp.where(col == cols - 1, 0.0, pltpu.roll(right, span - 1, 0))
    return left + middle + right


def padded_frame(edge_ref, middle_ref, mate_ref, cross_ref, f):
    above, below = rims(mate_ref, cross_ref, f)
    return jnp.concatenate([above, *frame_rows(edge_ref, middle_ref, f), below], axis=0)


def own_kernel(edge_ref, early_ref, late_ref, mate_ref, cross_ref, weight_ref, part_ref):
    cols, chans = edge_ref.shape[2:]
    span = part_ref.shape[0] // 2
    early = stacked_rows(padded_frame(edge_ref, early_ref, mate_ref, cross_ref, 0), 0, span, cols)
    late = stacked_rows(padded_frame(edge_ref, late_ref, mate_ref, cross_ref, 1), 0, span, cols)
    part_ref[:span] = joined_columns(column_taps([early], weight_ref, [2], chans), cols)
    part_ref[span:] = joined_columns(column_taps([early, late], weight_ref, [1, 2], chans), cols)


def older_terms(wide, start, span, weight_ref, time, cols):
    stack = stacked_rows(wide, start, span, cols)
    terms = joined_columns(column_taps([stack], weight_ref, [time], wide.shape[1]), cols)
    return jnp.where(lax.axis_index("tm") == 0, 0.0, terms)


def chunks_of(span, cols):
    size = span // 2 if span % (2 * cols) == 0 else span
    return [(start, size) for start in range(0, span, size)]


def features_of(conv, own, gain_ref):
    mean = jnp.mean(conv * conv, axis=1, keepdims=True)
    normed = conv * lax.rsqrt(mean + 1e-06) * gain_ref[...]
    silu = 0.5 * normed * (1.0 + jnp.tanh(0.5 * normed))
    return (own.astype(F32) + silu).astype(BF16)


def moments(features, targets):
    both = jnp.concatenate([features, targets], axis=1)
    return jnp.dot(features.T, both, preferred_element_type=F32)


def late_kernel(edge_ref, late_ref, old_edge_ref, old_late_ref, cross_ref, mate_ref, weight_ref, part_ref, gain_ref,
                target_ref, feature_ref, more_ref, sums_ref):
    cols, chans = edge_ref.shape[2:]
    span = part_ref.shape[0] // 2
    wide = padded_frame(old_edge_ref, old_late_ref, mate_ref, cross_ref, 1)
    own = jnp.concatenate(frame_rows(edge_ref, late_ref, 1), axis=0)
    chunks = chunks_of(span, cols)
    older = [older_terms(wide, start, size, weight_ref, 0, cols) for start, size in chunks]
    more_ref[...] = part_ref[:span] + older_terms(wide, 0, span, weight_ref, 1, cols)
    sums = jnp.zeros(sums_ref.shape, F32)
    for (start, size), terms in zip(chunks, older):
        conv = part_ref[span + start : span + start + size] + terms
        features = features_of(conv, own[start : start + size], gain_ref)
        feature_ref[start : start + size] = features
        sums = sums + moments(features, target_ref[span + start : span + start + size])
    sums_ref[...] = sums


def early_kernel(edge_ref, early_ref, old_edge_ref, old_early_ref, cross_ref, mate_ref, weight_ref, more_ref, sums_ref,
                 gain_ref, target_ref, feature_ref, keep_ref, send_ref):
    cols, chans = edge_ref.shape[2:]
    span, half = more_ref.shape[0], chans // 2
    wide = padded_frame(old_edge_ref, old_early_ref, mate_ref, cross_ref, 0)
    own = jnp.concatenate(frame_rows(edge_ref, early_ref, 0), axis=0)
    chunks = chunks_of(span, cols)
    older = [older_terms(wide, start, size, weight_ref, 0, cols) for start, size in chunks]
    sums = sums_ref[...]
    for (start, size), terms in zip(chunks, older):
        features = features_of(more_ref[start : start + size] + terms, own[start : start + size], gain_ref)
        feature_ref[start : start + size] = features
        sums = sums + moments(features, target_ref[start : start + size])
    row = lax.broadcasted_iota(jnp.int32, (half, half), 0)
    col = lax.broadcasted_iota(jnp.int32, (half, half), 1)
    head, tail = sums[:half, :half], sums[half:, half:chans]
    diagonal = jnp.sum(jnp.where(row == col, tail, 0.0), axis=0, keepdims=True)
    extra = jnp.concatenate([diagonal, jnp.zeros((HEAD // 2 - 1, half), F32)], axis=0)
    low = jnp.concatenate([jnp.where(row <= col, head, tail), sums[:half, half:chans], extra], axis=0)
    high = jnp.concatenate([sums[:half, chans:], sums[half:, chans:], jnp.zeros_like(extra)], axis=0)

    @pl.when(has_low())
    def _():
        keep_ref[...] = low
        send_ref[...] = high

    @pl.when(jnp.logical_not(has_low()))
    def _():
        keep_ref[...] = high
        send_ref[...] = low


def unpack_kernel(count, mine_ref, other_ref, gram_ref, cross_ref):
    half = mine_ref.shape[1]
    row = lax.broadcasted_iota(jnp.int32, (half, half), 0)
    col = lax.broadcasted_iota(jnp.int32, (half, half), 1)

    def fill(low, high):
        mixed, corner = low[:half] / count, low[half : 2 * half] / count
        diagonal = low[2 * half : 2 * half + 1] / count
        flipped = mixed.T
        gram_ref[:half, :half] = jnp.where(row <= col, mixed, flipped)
        gram_ref[:half, half:] = corner
        gram_ref[half:, :half] = corner.T
        gram_ref[half:, half:] = jnp.where(row > col, mixed, jnp.where(row == col, diagonal, flipped))
        cross_ref[...] = high[: 2 * half] / count

    @pl.when(has_low())
    def _():
        fill(mine_ref, other_ref)

    @pl.when(jnp.logical_not(has_low()))
    def _():
        fill(other_ref, mine_ref)


def places(mesh_axes=("tm", "row")):
    blocks, rows = (lax.axis_size(axis) for axis in mesh_axes)
    return [(a, b) for a in range(blocks) for b in range(rows)]


def with_mate(value):
    return by_device(value, [((a, b), (a, b ^ 1)) for a, b in places()])


def pack_kernel(keep_ref, got_ref, scaled_ref):
    rows, lanes = keep_ref.shape
    value = keep_ref[...] + got_ref[...]
    most = jnp.max(jnp.max(jnp.abs(value), axis=0, keepdims=True), axis=1, keepdims=True)
    exponent = jnp.floor(jnp.log2(jnp.maximum(most, 1e-30))) - 12.0
    scaled_ref[:rows] = value * jnp.exp2(-exponent)
    scaled_ref[rows:] = jnp.broadcast_to(exponent, (HEAD // 2, lanes))


def power(exponent):
    return lax.reduce_precision(jnp.exp2(exponent), 8, 7)


def joined_messages(messages, last):
    rows = messages[0].shape[0] - HEAD // 2
    exponents = [message[rows : rows + 1].astype(F32) for message in messages]
    messages = [message.astype(F32) for message in messages]
    e = functools.reduce(jnp.maximum, exponents) + len(messages) // 2
    if last:
        terms = [message[:rows] * power(p) for message, p in zip(messages, exponents)]
    else:
        terms = [message * power(p - e) for message, p in zip(messages, exponents)]
    while len(terms) > 1:
        terms = [a + b for a, b in zip(terms[::2], terms[1::2])]
    if last:
        return terms[0]
    row = lax.broadcasted_iota(jnp.int32, terms[0].shape, 0)
    return jnp.where(row < rows, terms[0], e).astype(F16)


def total_over_chips(keep, got):
    rounds = rounds_of_flips()
    size, lanes = keep.shape
    value = pl.pallas_call(
        pack_kernel,
        out_shape=jax.ShapeDtypeStruct((size + HEAD // 2, lanes), F32),
        in_specs=[WHOLE] * 2,
        out_specs=WHOLE,
        compiler_params=params(4),
    )(keep, got).astype(F16)
    for s, flips in enumerate(rounds):
        value = lax.optimization_barrier(value)
        other = rounds[s ^ 1] if s ^ 1 < len(rounds) and len(rounds[s ^ 1]) == len(flips) else flips
        messages = [value]
        for pair in zip(flips, other):
            moves = []
            for a, b in places():
                c, d = pair[side(a, b)]
                moves.append(((a, b), (a ^ c, b ^ d ^ side(c, d))))
            messages.append(by_device(value, moves))
        order = messages[::-1] if s == len(rounds) - 1 else [value, *messages[1:]]
        value = joined_messages(order, s == len(rounds) - 1)
    return value


def on_device(latents, conv_weight, norm_gain, depth_target):
    frames, rows, cols, chans = latents.shape
    spots = frames * rows * cols
    bins = depth_target.shape[3]
    half = chans // 2
    blocks, bands = lax.axis_size("tm"), lax.axis_size("row")
    rim = jax.ShapeDtypeStruct((frames, cols, chans), BF16)
    middle = jax.ShapeDtypeStruct((rows - 2, cols, chans), BF16)
    edge = latents[:, :: rows - 1]
    early, late, to_mate, to_cross = pl.pallas_call(
        cut_kernel,
        out_shape=(middle, middle, rim, rim),
        in_specs=[WHOLE] * 2,
        out_specs=(WHOLE,) * 4,
        compiler_params=params(4),
    )(latents, edge)
    old_edge, old_late, old_early = later(edge), later(late), later(early)
    mate, cross = with_mate(to_mate), with_neighbour(to_cross)
    old_to_mate, old_to_cross = pl.pallas_call(
        pick_kernel,
        out_shape=(rim, rim),
        in_specs=[WHOLE],
        out_specs=(WHOLE,) * 2,
        compiler_params=params(4),
        cost_estimate=pl.CostEstimate(flops=2 * 10**9, bytes_accessed=2**20, transcendentals=0),
    )(old_edge)
    old_mate, old_cross = with_mate(old_to_mate), with_neighbour(old_to_cross)
    part = pl.pallas_call(
        own_kernel,
        out_shape=jax.ShapeDtypeStruct((spots, chans), F32),
        in_specs=[WHOLE] * 6,
        out_specs=WHOLE,
        compiler_params=params(24),
        cost_estimate=pl.CostEstimate(flops=spots * chans * chans * 27, bytes_accessed=5 * 2**20, transcendentals=0),
    )(edge, early, late, mate, cross, conv_weight)
    gain, targets = norm_gain.reshape(1, chans), depth_target.reshape(spots, bins)
    half_features = jax.ShapeDtypeStruct((spots // 2, chans), BF16)
    late_features, more, sums = pl.pallas_call(
        late_kernel,
        out_shape=(
            half_features,
            jax.ShapeDtypeStruct((spots // 2, chans), F32),
            jax.ShapeDtypeStruct((chans, chans + bins), F32),
        ),
        in_specs=[WHOLE] * 10,
        out_specs=(WHOLE,) * 3,
        compiler_params=params(24),
        cost_estimate=pl.CostEstimate(flops=spots * chans * chans * 20, bytes_accessed=5 * 2**20, transcendentals=spots * chans // 2),
    )(edge, late, old_edge, old_late, old_cross, old_mate, conv_weight, part, gain, targets)
    share = jax.ShapeDtypeStruct((2 * half + HEAD // 2, half), F32)
    early_features, keep, send = pl.pallas_call(
        early_kernel,
        out_shape=(half_features, share, share),
        in_specs=[WHOLE] * 11,
        out_specs=(WHOLE,) * 3,
        compiler_params=params(24),
        cost_estimate=pl.CostEstimate(flops=spots * chans * chans * 10, bytes_accessed=5 * 2**20, transcendentals=spots * chans // 2),
    )(edge, early, old_edge, old_early, old_cross, old_mate, conv_weight, more, sums, gain, targets)
    features = jnp.stack([early_features, late_features])
    mine = total_over_chips(keep, with_mate(send))
    mine, features = lax.optimization_barrier((mine, features))
    other = with_mate(mine)
    gram, cross = pl.pallas_call(
        functools.partial(unpack_kernel, spots * blocks * bands),
        out_shape=(jax.ShapeDtypeStruct((chans, chans), F32), jax.ShapeDtypeStruct((chans, bins), F32)),
        in_specs=[WHOLE] * 2,
        out_specs=(WHOLE,) * 2,
        compiler_params=params(4),
    )(mine, other)
    return features.reshape(latents.shape), gram, cross


def solution(mesh):
    in_specs = (P("tm", "row", None, None), P(), P(), P("tm", "row", None, None))
    out_specs = (P("tm", "row", None, None), P(), P())
    return jax.shard_map(
        on_device, mesh=mesh, in_specs=in_specs, out_specs=out_specs, check_vma=False
    )
```

```python
import functools

import jax
import jax.numpy as jnp
from jax import lax
from jax.experimental import pallas as pl
from jax.experimental.pallas import tpu as pltpu
from jax.sharding import PartitionSpec as P

F32 = jnp.float32
BF16 = jnp.bfloat16
F16 = jnp.float16
HEAD = 16
WHOLE = pl.BlockSpec(memory_space=pltpu.VMEM)


def params(mebibytes):
    return pltpu.CompilerParams(vmem_limit_bytes=mebibytes * 2**20)


def on_even_row():
    return lax.axis_index("row") % 2 == 0


def odd_bits(value):
    for shift in (8, 4, 2, 1):
        value = value ^ (value >> shift)
    return value & 1


def rounds_of_flips():
    blocks, rows = lax.axis_size("tm"), lax.axis_size("row")
    bits = [(0, 2**k) for k in range(1, rows.bit_length() - 1)]
    bits += [(2**k, 0) for k in range(blocks.bit_length() - 1)]
    rounds = []
    for i in range(0, len(bits), 2):
        flips = bits[i : i + 2]
        if len(flips) == 2:
            flips.append((flips[0][0] ^ flips[1][0], flips[0][1] ^ flips[1][1]))
        rounds.append(flips)
    return rounds


def side(a, b):
    counted = [flips[min(1, len(flips) - 1)] for flips in rounds_of_flips()]
    tm, row = sum(c for c, _ in counted), 1 + sum(d for _, d in counted)
    return odd_bits(a & tm) ^ odd_bits(b & row)


def has_low():
    return side(lax.axis_index("tm"), lax.axis_index("row")) == 0


def by_device(value, moves):
    rows = lax.axis_size("row")
    return lax.ppermute(value, ("tm", "row"), [(a * rows + b, c * rows + d) for (a, b), (c, d) in moves])


def later(value):
    count = lax.axis_size("tm")
    return lax.ppermute(value, "tm", [(i, (i + 1) % count) for i in range(count)])


def cut_kernel(latents_ref, early_ref, late_ref):
    last = latents_ref.shape[1] - 1
    early_ref[...] = latents_ref[0, 1:last]
    late_ref[...] = latents_ref[1, 1:last]


def pick_kernel(edge_ref, mate_ref, cross_ref):
    def fill(to_mate, to_cross):
        mate_ref[...] = edge_ref[:, to_mate]
        cross_ref[...] = edge_ref[:, to_cross]

    @pl.when(on_even_row())
    def _():
        fill(1, 0)

    @pl.when(jnp.logical_not(on_even_row()))
    def _():
        fill(0, 1)


def picked(edge):
    frames, _, cols, chans = edge.shape
    rim = jax.ShapeDtypeStruct((frames, cols, chans), BF16)
    return pl.pallas_call(
        pick_kernel,
        out_shape=(rim, rim),
        in_specs=[WHOLE],
        out_specs=(WHOLE,) * 2,
        compiler_params=params(4),
        cost_estimate=pl.CostEstimate(flops=2 * 10**9, bytes_accessed=2**20, transcendentals=0),
    )(edge)


def with_neighbour(value):
    bands = lax.axis_size("row")
    return by_device(value, [((a, b), (a, (((b + 1) ^ 1) - 1) % bands)) for a, b in places()])


def rims(mate_ref, cross_ref, f):
    even = on_even_row()
    band = lax.axis_index("row")
    at_end = (band == 0) | (band == lax.axis_size("row") - 1)
    mate, cross = mate_ref[f], cross_ref[f]
    cross = jnp.where(at_end, jnp.zeros_like(cross), cross)
    return jnp.where(even, cross, mate), jnp.where(even, mate, cross)


def frame_rows(edge_ref, middle_ref, f):
    rows, cols, chans = middle_ref.shape
    return [edge_ref[f, 0], middle_ref[...].reshape(rows * cols, chans), edge_ref[f, 1]]


def column_taps(stacks, weight_ref, times, chans):
    rows = jnp.concatenate(stacks, axis=1)
    products = []
    for tap in range(3):
        weights = [weight_ref[t, dh, tap * chans : (tap + 1) * chans] for t in times for dh in range(3)]
        products.append(jnp.dot(rows, jnp.concatenate(weights, axis=0), preferred_element_type=F32))
    return products


def stacked_rows(wide, start, span, cols):
    return jnp.concatenate([wide[start + tap * cols : start + tap * cols + span] for tap in range(3)], axis=1)


def joined_columns(products, cols):
    left, middle, right = products
    span = left.shape[0]
    col = lax.broadcasted_iota(jnp.int32, (span, 1), 0) % cols
    left = jnp.where(col == 0, 0.0, pltpu.roll(left, 1, 0))
    right = jnp.where(col == cols - 1, 0.0, pltpu.roll(right, span - 1, 0))
    return left + middle + right


def padded_frame(edge_ref, middle_ref, mate_ref, cross_ref, f):
    above, below = rims(mate_ref, cross_ref, f)
    return jnp.concatenate([above, *frame_rows(edge_ref, middle_ref, f), below], axis=0)


def own_kernel(edge_ref, early_ref, late_ref, mate_ref, cross_ref, weight_ref, part_ref):
    cols, chans = edge_ref.shape[2:]
    span = part_ref.shape[0] // 2
    early = stacked_rows(padded_frame(edge_ref, early_ref, mate_ref, cross_ref, 0), 0, span, cols)
    late = stacked_rows(padded_frame(edge_ref, late_ref, mate_ref, cross_ref, 1), 0, span, cols)
    part_ref[:span] = joined_columns(column_taps([early], weight_ref, [2], chans), cols)
    part_ref[span:] = joined_columns(column_taps([early, late], weight_ref, [1, 2], chans), cols)


def older_terms(wide, start, span, weight_ref, time, cols):
    stack = stacked_rows(wide, start, span, cols)
    terms = joined_columns(column_taps([stack], weight_ref, [time], wide.shape[1]), cols)
    return jnp.where(lax.axis_index("tm") == 0, 0.0, terms)


def chunks_of(span, cols):
    size = span // 2 if span % (2 * cols) == 0 else span
    return [(start, size) for start in range(0, span, size)]


def features_of(conv, own, gain_ref):
    mean = jnp.mean(conv * conv, axis=1, keepdims=True)
    normed = conv * lax.rsqrt(mean + 1e-06) * gain_ref[...]
    silu = 0.5 * normed * (1.0 + jnp.tanh(0.5 * normed))
    return (own.astype(F32) + silu).astype(BF16)


def moments(features, targets):
    both = jnp.concatenate([features, targets], axis=1)
    return jnp.dot(features.T, both, preferred_element_type=F32)


def late_kernel(edge_ref, late_ref, old_edge_ref, old_late_ref, cross_ref, mate_ref, weight_ref, part_ref, gain_ref,
                target_ref, feature_ref, more_ref, sums_ref):
    cols, chans = edge_ref.shape[2:]
    span = part_ref.shape[0] // 2
    wide = padded_frame(old_edge_ref, old_late_ref, mate_ref, cross_ref, 1)
    own = jnp.concatenate(frame_rows(edge_ref, late_ref, 1), axis=0)
    chunks = chunks_of(span, cols)
    older = [older_terms(wide, start, size, weight_ref, 0, cols) for start, size in chunks]
    more_ref[...] = part_ref[:span] + older_terms(wide, 0, span, weight_ref, 1, cols)
    sums = jnp.zeros(sums_ref.shape, F32)
    for (start, size), terms in zip(chunks, older):
        conv = part_ref[span + start : span + start + size] + terms
        features = features_of(conv, own[start : start + size], gain_ref)
        feature_ref[start : start + size] = features
        sums = sums + moments(features, target_ref[span + start : span + start + size])
    sums_ref[...] = sums


def early_kernel(edge_ref, early_ref, old_edge_ref, old_early_ref, cross_ref, mate_ref, weight_ref, more_ref, sums_ref,
                 gain_ref, target_ref, feature_ref, keep_ref, send_ref):
    cols, chans = edge_ref.shape[2:]
    span, half = more_ref.shape[0], chans // 2
    wide = padded_frame(old_edge_ref, old_early_ref, mate_ref, cross_ref, 0)
    own = jnp.concatenate(frame_rows(edge_ref, early_ref, 0), axis=0)
    chunks = chunks_of(span, cols)
    older = [older_terms(wide, start, size, weight_ref, 0, cols) for start, size in chunks]
    sums = sums_ref[...]
    for (start, size), terms in zip(chunks, older):
        features = features_of(more_ref[start : start + size] + terms, own[start : start + size], gain_ref)
        feature_ref[start : start + size] = features
        sums = sums + moments(features, target_ref[start : start + size])
    row = lax.broadcasted_iota(jnp.int32, (half, half), 0)
    col = lax.broadcasted_iota(jnp.int32, (half, half), 1)
    head, tail = sums[:half, :half], sums[half:, half:chans]
    diagonal = jnp.sum(jnp.where(row == col, tail, 0.0), axis=0, keepdims=True)
    extra = jnp.concatenate([diagonal, jnp.zeros((HEAD // 2 - 1, half), F32)], axis=0)
    low = jnp.concatenate([jnp.where(row <= col, head, tail), sums[:half, half:chans], extra], axis=0)
    high = jnp.concatenate([sums[:half, chans:], sums[half:, chans:], jnp.zeros_like(extra)], axis=0)

    @pl.when(has_low())
    def _():
        keep_ref[...] = low
        send_ref[...] = high

    @pl.when(jnp.logical_not(has_low()))
    def _():
        keep_ref[...] = high
        send_ref[...] = low


def unpack_kernel(count, mine_ref, other_ref, gram_ref, cross_ref):
    half = mine_ref.shape[1]
    row = lax.broadcasted_iota(jnp.int32, (half, half), 0)
    col = lax.broadcasted_iota(jnp.int32, (half, half), 1)

    def fill(low, high):
        mixed, corner = low[:half] / count, low[half : 2 * half] / count
        diagonal = low[2 * half : 2 * half + 1] / count
        flipped = mixed.T
        gram_ref[:half, :half] = jnp.where(row <= col, mixed, flipped)
        gram_ref[:half, half:] = corner
        gram_ref[half:, :half] = corner.T
        gram_ref[half:, half:] = jnp.where(row > col, mixed, jnp.where(row == col, diagonal, flipped))
        cross_ref[...] = high[: 2 * half] / count

    @pl.when(has_low())
    def _():
        fill(mine_ref, other_ref)

    @pl.when(jnp.logical_not(has_low()))
    def _():
        fill(other_ref, mine_ref)


def places(mesh_axes=("tm", "row")):
    blocks, rows = (lax.axis_size(axis) for axis in mesh_axes)
    return [(a, b) for a in range(blocks) for b in range(rows)]


def with_mate(value):
    return by_device(value, [((a, b), (a, b ^ 1)) for a, b in places()])


def pack_kernel(keep_ref, got_ref, scaled_ref):
    rows, lanes = keep_ref.shape
    value = keep_ref[...] + got_ref[...]
    most = jnp.max(jnp.max(jnp.abs(value), axis=0, keepdims=True), axis=1, keepdims=True)
    exponent = jnp.floor(jnp.log2(jnp.maximum(most, 1e-30))) - 12.0
    scaled_ref[:rows] = value * jnp.exp2(-exponent)
    scaled_ref[rows:] = jnp.broadcast_to(exponent, (HEAD // 2, lanes))


def power(exponent):
    return lax.reduce_precision(jnp.exp2(exponent), 8, 7)


def joined_messages(messages, last):
    rows = messages[0].shape[0] - HEAD // 2
    exponents = [message[rows : rows + 1].astype(F32) for message in messages]
    messages = [message.astype(F32) for message in messages]
    e = functools.reduce(jnp.maximum, exponents) + len(messages) // 2
    if last:
        terms = [message[:rows] * power(p) for message, p in zip(messages, exponents)]
    else:
        terms = [message * power(p - e) for message, p in zip(messages, exponents)]
    while len(terms) > 1:
        terms = [a + b for a, b in zip(terms[::2], terms[1::2])]
    if last:
        return terms[0]
    row = lax.broadcasted_iota(jnp.int32, terms[0].shape, 0)
    return jnp.where(row < rows, terms[0], e).astype(F16)


def total_over_chips(keep, got):
    rounds = rounds_of_flips()
    size, lanes = keep.shape
    value = pl.pallas_call(
        pack_kernel,
        out_shape=jax.ShapeDtypeStruct((size + HEAD // 2, lanes), F32),
        in_specs=[WHOLE] * 2,
        out_specs=WHOLE,
        compiler_params=params(4),
    )(keep, got).astype(F16)
    for s, flips in enumerate(rounds):
        value = lax.optimization_barrier(value)
        other = rounds[s ^ 1] if s ^ 1 < len(rounds) and len(rounds[s ^ 1]) == len(flips) else flips
        messages = [value]
        for pair in zip(flips, other):
            moves = []
            for a, b in places():
                c, d = pair[side(a, b)]
                moves.append(((a, b), (a ^ c, b ^ d ^ side(c, d))))
            messages.append(by_device(value, moves))
        order = messages[::-1] if s == len(rounds) - 1 else [value, *messages[1:]]
        value = joined_messages(order, s == len(rounds) - 1)
    return value


def on_device(latents, conv_weight, norm_gain, depth_target):
    frames, rows, cols, chans = latents.shape
    spots = frames * rows * cols
    bins = depth_target.shape[3]
    half = chans // 2
    blocks, bands = lax.axis_size("tm"), lax.axis_size("row")
    middle = jax.ShapeDtypeStruct((rows - 2, cols, chans), BF16)
    edge = latents[:, :: rows - 1]
    to_mate, to_cross = picked(edge)
    early, late = pl.pallas_call(
        cut_kernel,
        out_shape=(middle, middle),
        in_specs=[WHOLE],
        out_specs=(WHOLE,) * 2,
        compiler_params=params(4),
    )(latents)
    old_edge, old_late, old_early = later(edge), later(late), later(early)
    mate, cross = with_mate(to_mate), with_neighbour(to_cross)
    old_to_mate, old_to_cross = picked(old_edge)
    old_mate, old_cross = with_mate(old_to_mate), with_neighbour(old_to_cross)
    part = pl.pallas_call(
        own_kernel,
        out_shape=jax.ShapeDtypeStruct((spots, chans), F32),
        in_specs=[WHOLE] * 6,
        out_specs=WHOLE,
        compiler_params=params(24),
        cost_estimate=pl.CostEstimate(flops=spots * chans * chans * 27, bytes_accessed=5 * 2**20, transcendentals=0),
    )(edge, early, late, mate, cross, conv_weight)
    gain, targets = norm_gain.reshape(1, chans), depth_target.reshape(spots, bins)
    half_features = jax.ShapeDtypeStruct((spots // 2, chans), BF16)
    late_features, more, sums = pl.pallas_call(
        late_kernel,
        out_shape=(
            half_features,
            jax.ShapeDtypeStruct((spots // 2, chans), F32),
            jax.ShapeDtypeStruct((chans, chans + bins), F32),
        ),
        in_specs=[WHOLE] * 10,
        out_specs=(WHOLE,) * 3,
        compiler_params=params(24),
        cost_estimate=pl.CostEstimate(flops=spots * chans * chans * 20, bytes_accessed=5 * 2**20, transcendentals=spots * chans // 2),
    )(edge, late, old_edge, old_late, old_cross, old_mate, conv_weight, part, gain, targets)
    share = jax.ShapeDtypeStruct((2 * half + HEAD // 2, half), F32)
    early_features, keep, send = pl.pallas_call(
        early_kernel,
        out_shape=(half_features, share, share),
        in_specs=[WHOLE] * 11,
        out_specs=(WHOLE,) * 3,
        compiler_params=params(24),
        cost_estimate=pl.CostEstimate(flops=spots * chans * chans * 10, bytes_accessed=5 * 2**20, transcendentals=spots * chans // 2),
    )(edge, early, old_edge, old_early, old_cross, old_mate, conv_weight, more, sums, gain, targets)
    features = jnp.stack([early_features, late_features])
    mine = total_over_chips(keep, with_mate(send))
    mine, features = lax.optimization_barrier((mine, features))
    other = with_mate(mine)
    gram, cross = pl.pallas_call(
        functools.partial(unpack_kernel, spots * blocks * bands),
        out_shape=(jax.ShapeDtypeStruct((chans, chans), F32), jax.ShapeDtypeStruct((chans, bins), F32)),
        in_specs=[WHOLE] * 2,
        out_specs=(WHOLE,) * 2,
        compiler_params=params(4),
    )(mine, other)
    return features.reshape(latents.shape), gram, cross


def solution(mesh):
    in_specs = (P("tm", "row", None, None), P(), P(), P("tm", "row", None, None))
    out_specs = (P("tm", "row", None, None), P(), P())
    return jax.shard_map(
        on_device, mesh=mesh, in_specs=in_specs, out_specs=out_specs, check_vma=False
    )
```

```python
import functools

import jax
import jax.numpy as jnp
from jax import lax
from jax.experimental import pallas as pl
from jax.experimental.pallas import tpu as pltpu
from jax.sharding import PartitionSpec as P

F32 = jnp.float32
BF16 = jnp.bfloat16
F16 = jnp.float16
HEAD = 16
WHOLE = pl.BlockSpec(memory_space=pltpu.VMEM)


def params(mebibytes):
    return pltpu.CompilerParams(vmem_limit_bytes=mebibytes * 2**20)


def on_even_row():
    return lax.axis_index("row") % 2 == 0


def odd_bits(value):
    for shift in (8, 4, 2, 1):
        value = value ^ (value >> shift)
    return value & 1


def rounds_of_flips():
    blocks, rows = lax.axis_size("tm"), lax.axis_size("row")
    bits = [(0, 2**k) for k in range(1, rows.bit_length() - 1)]
    bits += [(2**k, 0) for k in range(blocks.bit_length() - 1)]
    rounds = []
    for i in range(0, len(bits), 2):
        flips = bits[i : i + 2]
        if len(flips) == 2:
            flips.append((flips[0][0] ^ flips[1][0], flips[0][1] ^ flips[1][1]))
        rounds.append(flips)
    return rounds


def side(a, b):
    counted = [flips[min(1, len(flips) - 1)] for flips in rounds_of_flips()]
    tm, row = sum(c for c, _ in counted), 1 + sum(d for _, d in counted)
    return odd_bits(a & tm) ^ odd_bits(b & row)


def has_low():
    return side(lax.axis_index("tm"), lax.axis_index("row")) == 0


def by_device(value, moves):
    rows = lax.axis_size("row")
    return lax.ppermute(value, ("tm", "row"), [(a * rows + b, c * rows + d) for (a, b), (c, d) in moves])


def later(value):
    count = lax.axis_size("tm")
    return lax.ppermute(value, "tm", [(i, (i + 1) % count) for i in range(count)])


def cut_kernel(latents_ref, early_ref, late_ref):
    last = latents_ref.shape[1] - 1
    early_ref[...] = latents_ref[0, 1:last]
    late_ref[...] = latents_ref[1, 1:last]


def pick_kernel(edge_ref, mate_ref, cross_ref):
    def fill(to_mate, to_cross):
        mate_ref[...] = edge_ref[:, to_mate]
        cross_ref[...] = edge_ref[:, to_cross]

    @pl.when(on_even_row())
    def _():
        fill(1, 0)

    @pl.when(jnp.logical_not(on_even_row()))
    def _():
        fill(0, 1)


def picked(edge):
    frames, _, cols, chans = edge.shape
    rim = jax.ShapeDtypeStruct((frames, cols, chans), BF16)
    return pl.pallas_call(
        pick_kernel,
        out_shape=(rim, rim),
        in_specs=[WHOLE],
        out_specs=(WHOLE,) * 2,
        compiler_params=params(4),
        cost_estimate=pl.CostEstimate(flops=2 * 10**9, bytes_accessed=2**20, transcendentals=0),
    )(edge)


def with_neighbour(value):
    bands = lax.axis_size("row")
    return by_device(value, [((a, b), (a, (((b + 1) ^ 1) - 1) % bands)) for a, b in places()])


def rims(mate_ref, cross_ref, f):
    even = on_even_row()
    band = lax.axis_index("row")
    at_end = (band == 0) | (band == lax.axis_size("row") - 1)
    mate, cross = mate_ref[f], cross_ref[f]
    cross = jnp.where(at_end, jnp.zeros_like(cross), cross)
    return jnp.where(even, cross, mate), jnp.where(even, mate, cross)


def frame_rows(edge_ref, middle_ref, f):
    rows, cols, chans = middle_ref.shape
    return [edge_ref[f, 0], middle_ref[...].reshape(rows * cols, chans), edge_ref[f, 1]]


def column_taps(stacks, weight_ref, times, chans):
    rows = jnp.concatenate(stacks, axis=1)
    products = []
    for tap in range(3):
        weights = [weight_ref[t, dh, tap * chans : (tap + 1) * chans] for t in times for dh in range(3)]
        products.append(jnp.dot(rows, jnp.concatenate(weights, axis=0), preferred_element_type=F32))
    return products


def stacked_rows(wide, start, span, cols):
    return jnp.concatenate([wide[start + tap * cols : start + tap * cols + span] for tap in range(3)], axis=1)


def joined_columns(products, cols):
    left, middle, right = products
    span = left.shape[0]
    col = lax.broadcasted_iota(jnp.int32, (span, 1), 0) % cols
    left = jnp.where(col == 0, 0.0, pltpu.roll(left, 1, 0))
    right = jnp.where(col == cols - 1, 0.0, pltpu.roll(right, span - 1, 0))
    return left + middle + right


def padded_frame(edge_ref, middle_ref, mate_ref, cross_ref, f):
    above, below = rims(mate_ref, cross_ref, f)
    return jnp.concatenate([above, *frame_rows(edge_ref, middle_ref, f), below], axis=0)


def own_kernel(edge_ref, early_ref, late_ref, cross_ref, mate_ref, weight_ref, part_ref):
    cols, chans = edge_ref.shape[2:]
    span = part_ref.shape[0] // 2
    early = stacked_rows(padded_frame(edge_ref, early_ref, mate_ref, cross_ref, 0), 0, span, cols)
    late = stacked_rows(padded_frame(edge_ref, late_ref, mate_ref, cross_ref, 1), 0, span, cols)
    part_ref[:span] = joined_columns(column_taps([early], weight_ref, [2], chans), cols)
    part_ref[span:] = joined_columns(column_taps([early, late], weight_ref, [1, 2], chans), cols)


def older_terms(wide, start, span, weight_ref, time, cols):
    stack = stacked_rows(wide, start, span, cols)
    terms = joined_columns(column_taps([stack], weight_ref, [time], wide.shape[1]), cols)
    return jnp.where(lax.axis_index("tm") == 0, 0.0, terms)


def chunks_of(span, cols):
    size = span // 2 if span % (2 * cols) == 0 else span
    return [(start, size) for start in range(0, span, size)]


def features_of(conv, own, gain_ref):
    mean = jnp.mean(conv * conv, axis=1, keepdims=True)
    normed = conv * lax.rsqrt(mean + 1e-06) * gain_ref[...]
    silu = 0.5 * normed * (1.0 + jnp.tanh(0.5 * normed))
    return (own.astype(F32) + silu).astype(BF16)


def moments(features, targets):
    both = jnp.concatenate([features, targets], axis=1)
    return jnp.dot(features.T, both, preferred_element_type=F32)


def late_kernel(edge_ref, late_ref, old_edge_ref, old_late_ref, cross_ref, mate_ref, weight_ref, part_ref, gain_ref,
                target_ref, feature_ref, more_ref, sums_ref):
    cols, chans = edge_ref.shape[2:]
    span = part_ref.shape[0] // 2
    wide = padded_frame(old_edge_ref, old_late_ref, mate_ref, cross_ref, 1)
    own = jnp.concatenate(frame_rows(edge_ref, late_ref, 1), axis=0)
    chunks = chunks_of(span, cols)
    older = [older_terms(wide, start, size, weight_ref, 0, cols) for start, size in chunks]
    more_ref[...] = part_ref[:span] + older_terms(wide, 0, span, weight_ref, 1, cols)
    sums = jnp.zeros(sums_ref.shape, F32)
    for (start, size), terms in zip(chunks, older):
        conv = part_ref[span + start : span + start + size] + terms
        features = features_of(conv, own[start : start + size], gain_ref)
        feature_ref[start : start + size] = features
        sums = sums + moments(features, target_ref[span + start : span + start + size])
    sums_ref[...] = sums


def early_kernel(edge_ref, early_ref, old_edge_ref, old_early_ref, cross_ref, mate_ref, weight_ref, more_ref, sums_ref,
                 gain_ref, target_ref, feature_ref, keep_ref, send_ref):
    cols, chans = edge_ref.shape[2:]
    span, half = more_ref.shape[0], chans // 2
    wide = padded_frame(old_edge_ref, old_early_ref, mate_ref, cross_ref, 0)
    own = jnp.concatenate(frame_rows(edge_ref, early_ref, 0), axis=0)
    chunks = chunks_of(span, cols)
    older = [older_terms(wide, start, size, weight_ref, 0, cols) for start, size in chunks]
    sums = sums_ref[...]
    for (start, size), terms in zip(chunks, older):
        features = features_of(more_ref[start : start + size] + terms, own[start : start + size], gain_ref)
        feature_ref[start : start + size] = features
        sums = sums + moments(features, target_ref[start : start + size])
    row = lax.broadcasted_iota(jnp.int32, (half, half), 0)
    col = lax.broadcasted_iota(jnp.int32, (half, half), 1)
    head, tail = sums[:half, :half], sums[half:, half:chans]
    diagonal = jnp.sum(jnp.where(row == col, tail, 0.0), axis=0, keepdims=True)
    extra = jnp.concatenate([diagonal, jnp.zeros((HEAD // 2 - 1, half), F32)], axis=0)
    low = jnp.concatenate([jnp.where(row <= col, head, tail), sums[:half, half:chans], extra], axis=0)
    high = jnp.concatenate([sums[:half, chans:], sums[half:, chans:], jnp.zeros_like(extra)], axis=0)

    @pl.when(has_low())
    def _():
        keep_ref[...] = low
        send_ref[...] = high

    @pl.when(jnp.logical_not(has_low()))
    def _():
        keep_ref[...] = high
        send_ref[...] = low


def unpack_kernel(count, mine_ref, other_ref, gram_ref, cross_ref):
    half = mine_ref.shape[1]
    row = lax.broadcasted_iota(jnp.int32, (half, half), 0)
    col = lax.broadcasted_iota(jnp.int32, (half, half), 1)

    def fill(low, high):
        mixed, corner = low[:half] / count, low[half : 2 * half] / count
        diagonal = low[2 * half : 2 * half + 1] / count
        flipped = mixed.T
        gram_ref[:half, :half] = jnp.where(row <= col, mixed, flipped)
        gram_ref[:half, half:] = corner
        gram_ref[half:, :half] = corner.T
        gram_ref[half:, half:] = jnp.where(row > col, mixed, jnp.where(row == col, diagonal, flipped))
        cross_ref[...] = high[: 2 * half] / count

    @pl.when(has_low())
    def _():
        fill(mine_ref, other_ref)

    @pl.when(jnp.logical_not(has_low()))
    def _():
        fill(other_ref, mine_ref)


def places(mesh_axes=("tm", "row")):
    blocks, rows = (lax.axis_size(axis) for axis in mesh_axes)
    return [(a, b) for a in range(blocks) for b in range(rows)]


def with_mate(value):
    return by_device(value, [((a, b), (a, b ^ 1)) for a, b in places()])


def pack_kernel(keep_ref, got_ref, scaled_ref):
    rows, lanes = keep_ref.shape
    value = keep_ref[...] + got_ref[...]
    most = jnp.max(jnp.max(jnp.abs(value), axis=0, keepdims=True), axis=1, keepdims=True)
    exponent = jnp.floor(jnp.log2(jnp.maximum(most, 1e-30))) - 12.0
    scaled_ref[:rows] = value * jnp.exp2(-exponent)
    scaled_ref[rows:] = jnp.broadcast_to(exponent, (HEAD // 2, lanes))


def power(exponent):
    return lax.reduce_precision(jnp.exp2(exponent), 8, 7)


def joined_messages(messages, last):
    rows = messages[0].shape[0] - HEAD // 2
    exponents = [message[rows : rows + 1].astype(F32) for message in messages]
    messages = [message.astype(F32) for message in messages]
    e = functools.reduce(jnp.maximum, exponents) + len(messages) // 2
    if last:
        terms = [message[:rows] * power(p) for message, p in zip(messages, exponents)]
    else:
        terms = [message * power(p - e) for message, p in zip(messages, exponents)]
    while len(terms) > 1:
        terms = [a + b for a, b in zip(terms[::2], terms[1::2])]
    if last:
        return terms[0]
    row = lax.broadcasted_iota(jnp.int32, terms[0].shape, 0)
    return jnp.where(row < rows, terms[0], e).astype(F16)


def total_over_chips(keep, got):
    rounds = rounds_of_flips()
    size, lanes = keep.shape
    value = pl.pallas_call(
        pack_kernel,
        out_shape=jax.ShapeDtypeStruct((size + HEAD // 2, lanes), F32),
        in_specs=[WHOLE] * 2,
        out_specs=WHOLE,
        compiler_params=params(4),
    )(keep, got).astype(F16)
    for s, flips in enumerate(rounds):
        value = lax.optimization_barrier(value)
        other = rounds[s ^ 1] if s ^ 1 < len(rounds) and len(rounds[s ^ 1]) == len(flips) else flips
        messages = [value]
        for pair in zip(flips, other):
            moves = []
            for a, b in places():
                c, d = pair[side(a, b)]
                moves.append(((a, b), (a ^ c, b ^ d ^ side(c, d))))
            messages.append(by_device(value, moves))
        order = messages[::-1] if s == len(rounds) - 1 else [value, *messages[1:]]
        value = joined_messages(order, s == len(rounds) - 1)
    return value


def on_device(latents, conv_weight, norm_gain, depth_target):
    frames, rows, cols, chans = latents.shape
    spots = frames * rows * cols
    bins = depth_target.shape[3]
    half = chans // 2
    blocks, bands = lax.axis_size("tm"), lax.axis_size("row")
    middle = jax.ShapeDtypeStruct((rows - 2, cols, chans), BF16)
    edge = latents[:, :: rows - 1]
    to_mate, to_cross = picked(edge)
    early, late = pl.pallas_call(
        cut_kernel,
        out_shape=(middle, middle),
        in_specs=[WHOLE],
        out_specs=(WHOLE,) * 2,
        compiler_params=params(4),
    )(latents)
    old_edge, old_late, old_early = later(edge), later(late), later(early)
    mate, cross = with_mate(to_mate), with_neighbour(to_cross)
    old_to_mate, old_to_cross = picked(old_edge)
    old_mate, old_cross = with_mate(old_to_mate), with_neighbour(old_to_cross)
    part = pl.pallas_call(
        own_kernel,
        out_shape=jax.ShapeDtypeStruct((spots, chans), F32),
        in_specs=[WHOLE] * 6,
        out_specs=WHOLE,
        compiler_params=params(24),
        cost_estimate=pl.CostEstimate(flops=spots * chans * chans * 27, bytes_accessed=5 * 2**20, transcendentals=0),
    )(edge, early, late, cross, mate, conv_weight)
    gain, targets = norm_gain.reshape(1, chans), depth_target.reshape(spots, bins)
    half_features = jax.ShapeDtypeStruct((spots // 2, chans), BF16)
    late_features, more, sums = pl.pallas_call(
        late_kernel,
        out_shape=(
            half_features,
            jax.ShapeDtypeStruct((spots // 2, chans), F32),
            jax.ShapeDtypeStruct((chans, chans + bins), F32),
        ),
        in_specs=[WHOLE] * 10,
        out_specs=(WHOLE,) * 3,
        compiler_params=params(24),
        cost_estimate=pl.CostEstimate(flops=spots * chans * chans * 20, bytes_accessed=5 * 2**20, transcendentals=spots * chans // 2),
    )(edge, late, old_edge, old_late, old_cross, old_mate, conv_weight, part, gain, targets)
    share = jax.ShapeDtypeStruct((2 * half + HEAD // 2, half), F32)
    early_features, keep, send = pl.pallas_call(
        early_kernel,
        out_shape=(half_features, share, share),
        in_specs=[WHOLE] * 11,
        out_specs=(WHOLE,) * 3,
        compiler_params=params(24),
        cost_estimate=pl.CostEstimate(flops=spots * chans * chans * 10, bytes_accessed=5 * 2**20, transcendentals=spots * chans // 2),
    )(edge, early, old_edge, old_early, old_cross, old_mate, conv_weight, more, sums, gain, targets)
    features = jnp.stack([early_features, late_features])
    mine = total_over_chips(keep, with_mate(send))
    mine, features = lax.optimization_barrier((mine, features))
    other = with_mate(mine)
    gram, cross = pl.pallas_call(
        functools.partial(unpack_kernel, spots * blocks * bands),
        out_shape=(jax.ShapeDtypeStruct((chans, chans), F32), jax.ShapeDtypeStruct((chans, bins), F32)),
        in_specs=[WHOLE] * 2,
        out_specs=(WHOLE,) * 2,
        compiler_params=params(4),
    )(mine, other)
    return features.reshape(latents.shape), gram, cross


def solution(mesh):
    in_specs = (P("tm", "row", None, None), P(), P(), P("tm", "row", None, None))
    out_specs = (P("tm", "row", None, None), P(), P())
    return jax.shard_map(
        on_device, mesh=mesh, in_specs=in_specs, out_specs=out_specs, check_vma=False
    )
```
